32 devices in a mesh: seq: 8 (over z, core), blk: 4 (over y, x).
Axes of the slice: x: 2, y: 2, z: 4, core: 2. Of those that a mesh axis runs over, the one named last changes fastest.
Arguments:
- queries: float32 [4096, 3072], P(('seq', 'blk')), may hold values from -8 to 8
- key_matrix: float32 [4096, 3072], P(('seq', 'blk')), may hold values from -8 to 8
- value_matrix: float32 [4096, 3072], P(('seq', 'blk')), may hold values from -6 to 6
- gate_logits: float32 [4096, 24], P(('seq', 'blk')), may hold values from -6 to 6
- output_grad: float32 [4096, 3072], P(('seq', 'blk')), may hold values from -6 to 6
- cycle_offsets: int32 [32, 4], P(('seq', 'blk')), may hold values from -2 to 2, as said below
- block_count: int32 [32], P(('seq', 'blk')), may hold values from 1 to 4
- feature_seed: int32 [128, 256], replicated, may hold values from -3 to 3
Outputs:
- attended: float32 [4096, 3072], P(('seq', 'blk'))
- query_grad: float32 [4096, 3072], P(('seq', 'blk'))
- key_grad: float32 [4096, 3072], P(('seq', 'blk'))
- value_grad: float32 [4096, 3072], P(('seq', 'blk'))
- gate_grad: float32 [4096, 24], P(('seq', 'blk'))
The draws below stay inside these ranges and needn't reach their ends.
Inputs may be any that keep to these rules, and one draw needn't show every extreme that they name: `cycle_offsets`: each row holds -2, -1, 1 and 2 once each.
All inputs are finite; a program needn't handle non-finite values.
Results may differ from the reference program's by a relative error of at most 0.0003.
Values sent between devices are 32-bit elements; how exact they have to be, the bound alone decides.
No kernel may reach another device: no remote copies, remote signals or barrier semaphores. Data moves between devices by JAX's collectives and lax.ppermute only.
A program may use at most 192 MiB of HBM per device.

```python
import math
import jax
import jax.numpy as jnp
from jax import lax

HEADS = 24
HEAD_DIM = 128
FEATURES = 256
TOK_DEV = 128
SLOTS = 4
REACH = 64
CYCLE = 4
QBLOCKS = 32
TOKENS = 4096
WIDTH = 3072


def draw_queries(key, part):
    key = jax.random.fold_in(key, 31)
    return jnp.clip(jax.random.normal(key, (TOKENS, WIDTH)), -8.0, 8.0).astype(jnp.float32)


def draw_key_matrix(key, part):
    key = jax.random.fold_in(key, 32)
    return jnp.clip(jax.random.normal(key, (TOKENS, WIDTH)), -8.0, 8.0).astype(jnp.float32)


def draw_cycle_offsets(key, part):
    key = jax.random.fold_in(key, 41)
    subkeys = jax.random.split(key, QBLOCKS)

    def shuffled(subkey):
        return jax.random.permutation(subkey, SLOTS)
    orders = jax.vmap(shuffled)(subkeys)
    table = jnp.array([-2, -1, 1, 2], dtype=jnp.int32)
    return table[orders].astype(jnp.int32)


def draw_block_count(key, part):
    key = jax.random.fold_in(key, 42)
    pick_key, place_key = jax.random.split(key)
    levels = jnp.array([4, 3, 2, 1, 1, 1, 1, 1, 1, 1, 1, 1], dtype=jnp.int32)
    counts = levels[jax.random.randint(pick_key, (QBLOCKS,), 0, 12)]
    busiest = jax.random.randint(place_key, (), 0, QBLOCKS)
    return counts.at[busiest].set(SLOTS).astype(jnp.int32)


def place_ends(values, stream_key, low, largest):
    longest = values.shape.index(max(values.shape))
    spots = []
    for shift in (0, 1):
        where = [jax.random.randint(jax.random.fold_in(stream_key, axis), (), 0, length) for axis, length in enumerate(values.shape)]
        where[longest] = (where[longest] + shift) % values.shape[longest]
        spots.append(tuple(where))
    return values.at[spots[0]].set(low).at[spots[1]].set(largest)


def shard_levels(key, shape, pieces, low, largest):
    level = 1.0
    for axis_at, shards_of in pieces:
        steps = jax.random.uniform(jax.random.fold_in(jax.random.fold_in(key, 6), axis_at), (shards_of,), jnp.float32, low / len(pieces), largest / len(pieces))
        level = level * jnp.repeat(jnp.exp(steps), shape[axis_at] // shards_of).reshape((-1,) + (1,) * (len(shape) - 1 - axis_at))
    return level


def scatter_about(own_key, extent, width, limit, pieces=(), kind=jnp.bfloat16):
    result = jax.random.normal(own_key, extent, jnp.float32) * width
    if len(pieces) > 0:
        result = shard_levels(own_key, extent, pieces, -0.22, 0.18) * result
    return jnp.clip(result, min=-limit, max=limit).astype(kind)


def setup_inputs(seed: int = 0) -> dict:
    arg_keys = jax.random.split(jax.random.key(seed), 9)
    queries = draw_queries(jax.random.fold_in(arg_keys[8], 71), 0)
    key_matrix = draw_key_matrix(jax.random.fold_in(arg_keys[8], 71), 0)
    value_matrix = scatter_about(arg_keys[2], (TOKENS, WIDTH), 1.0, 6.0, ((0, 32),), jnp.float32)
    gate_logits = scatter_about(arg_keys[3], (TOKENS, HEADS), 2.0, 6.0, ((0, 32),), jnp.float32)
    output_grad = scatter_about(arg_keys[4], (TOKENS, WIDTH), 1.0, 6.0, ((0, 32),), jnp.float32)
    cycle_offsets = draw_cycle_offsets(jax.random.fold_in(arg_keys[8], 71), 0)
    block_count = draw_block_count(jax.random.fold_in(arg_keys[8], 71), 0)
    feature_seed = place_ends(jax.random.randint(arg_keys[7], (HEAD_DIM, FEATURES), -3, 4), jax.random.fold_in(arg_keys[7], 1), -3, 3).astype(jnp.int32)
    return {"queries": queries, "key_matrix": key_matrix, "value_matrix": value_matrix, "gate_logits": gate_logits, "output_grad": output_grad, "cycle_offsets": cycle_offsets, "block_count": block_count, "feature_seed": feature_seed}


HIGH = lax.Precision.HIGHEST
CANDIDATES = (1, -1, 2, -2)
NEG_FILL = -1e+30

def feature_map(heads_in, projection):
    normed = heads_in * lax.rsqrt(lax.optimization_barrier(jnp.mean(heads_in * heads_in, axis=-1, keepdims=True)) + 1e-06)
    return jnp.exp(jnp.einsum('nhd,df->nhf', normed, projection, precision=HIGH))

def used_flags(offsets, used_count, cycle_size):
    active = jnp.arange(offsets.shape[0], dtype=jnp.int32) < used_count
    residues = jnp.mod(offsets, cycle_size)
    flag_list = []
    for position, candidate in enumerate(CANDIDATES):
        residue = candidate % cycle_size
        earlier = any((previous % cycle_size == residue for previous in CANDIDATES[:position]))
        chosen = jnp.any(active & (residues == residue))
        flag_list.append(jnp.logical_and(chosen, not earlier))
    return flag_list

def sparse_block(query_rows, key_rows, value_rows, allowed):
    heads_num = query_rows.shape[1] // HEAD_DIM
    query_heads = query_rows.reshape(query_rows.shape[0], heads_num, HEAD_DIM)
    key_heads = key_rows.reshape(key_rows.shape[0], heads_num, HEAD_DIM)
    value_heads = value_rows.reshape(value_rows.shape[0], heads_num, HEAD_DIM)
    scores = jnp.einsum('ihd,jhd->hij', query_heads, key_heads, precision=HIGH) / math.sqrt(HEAD_DIM)
    scores = jnp.where(allowed[None] > 0.0, scores, NEG_FILL)
    highest = lax.stop_gradient(lax.optimization_barrier(jnp.max(scores, axis=-1, keepdims=True)))
    weights = jnp.exp(scores - highest) * allowed[None]
    totals = lax.optimization_barrier(jnp.sum(weights, axis=-1))
    mixed = jnp.einsum('hij,jhd->ihd', weights, value_heads, precision=HIGH)
    return (mixed / jnp.transpose(totals)[:, :, None]).reshape(query_rows.shape[0], -1)

def split_heads(matrix):
    return matrix.reshape(matrix.shape[0], HEADS, HEAD_DIM)

def attention_layer(queries, key_matrix, value_matrix, gate_logits, cycle_offsets, block_count, feature_seed):
    projection = feature_seed.astype(jnp.float32) / 13.0
    query_feats = feature_map(split_heads(queries), projection)
    key_feats = feature_map(split_heads(key_matrix), projection)
    kv_sums = jnp.einsum('nhf,nhd->hfd', key_feats, split_heads(value_matrix), precision=HIGH)
    key_totals = lax.optimization_barrier(jnp.sum(key_feats, axis=0))
    numerator = jnp.einsum('nhf,hfd->nhd', query_feats, kv_sums, precision=HIGH)
    denominator = jnp.einsum('nhf,hf->nh', query_feats, key_totals, precision=HIGH)
    low_rank = numerator / denominator[:, :, None]
    pad_keys = jnp.pad(key_matrix, ((REACH, REACH), (0, 0)))
    pad_values = jnp.pad(value_matrix, ((REACH, REACH), (0, 0)))

    def one_block(block_index):
        row_start = block_index * TOK_DEV
        query_rows = lax.dynamic_slice_in_dim(queries, row_start, TOK_DEV, 0)
        key_list = [lax.dynamic_slice_in_dim(pad_keys, row_start, TOK_DEV + 2 * REACH, 0)]
        value_list = [lax.dynamic_slice_in_dim(pad_values, row_start, TOK_DEV + 2 * REACH, 0)]
        query_pos = row_start + jnp.arange(TOK_DEV, dtype=jnp.int32)
        near_pos = row_start - REACH + jnp.arange(TOK_DEV + 2 * REACH, dtype=jnp.int32)
        near_gap = jnp.abs(near_pos[None, :] - query_pos[:, None])
        allowed_list = [(near_gap <= REACH) & (near_pos >= 0)[None, :] & (near_pos < TOKENS)[None, :]]
        member = jnp.mod(block_index, CYCLE)
        flag_list = used_flags(cycle_offsets[block_index], block_count[block_index], CYCLE)
        for candidate, tile_flag in zip(CANDIDATES, flag_list):
            source = block_index - member + jnp.mod(member + candidate, CYCLE)
            tile_start = (source * TOK_DEV).astype(jnp.int32)
            key_list.append(lax.dynamic_slice_in_dim(key_matrix, tile_start, TOK_DEV, 0))
            value_list.append(lax.dynamic_slice_in_dim(value_matrix, tile_start, TOK_DEV, 0))
            tile_pos = tile_start + jnp.arange(TOK_DEV, dtype=jnp.int32)
            allowed_list.append(tile_flag & (jnp.abs(tile_pos[None, :] - query_pos[:, None]) > REACH))
        allowed = jnp.concatenate(allowed_list, axis=1).astype(jnp.float32)
        return sparse_block(query_rows, jnp.concatenate(key_list, axis=0), jnp.concatenate(value_list, axis=0), allowed)
    sparse = lax.map(jax.checkpoint(one_block), jnp.arange(QBLOCKS, dtype=jnp.int32))
    sparse = sparse.reshape(TOKENS, HEADS, HEAD_DIM)
    gate = jax.nn.sigmoid(gate_logits)[:, :, None]
    mixed = gate * sparse + (1.0 - gate) * low_rank
    return mixed.reshape(TOKENS, WIDTH)

def reference(queries, key_matrix, value_matrix, gate_logits, output_grad, cycle_offsets, block_count, feature_seed):

    def closed_layer(query_in, key_in, value_in, gate_in):
        return attention_layer(query_in, key_in, value_in, gate_in, cycle_offsets, block_count, feature_seed)
    attended, pullback = jax.vjp(closed_layer, queries, key_matrix, value_matrix, gate_logits)
    query_grad, key_grad, value_grad, gate_grad = pullback(output_grad)
    return (attended, query_grad, key_grad, value_grad, gate_grad)
```

```python
import functools
import math

import jax
import jax.numpy as jnp
from jax import lax
from jax.experimental import pallas as pl
from jax.experimental.pallas import tpu as pltpu
from jax.sharding import PartitionSpec as P

HEAD_DIM = 128
EXT = 8
NEG_FILL = -1e30
SEED_DIV = 13.0
EPS = 1e-06
F32 = jnp.float32
BF16 = jnp.bfloat16


def split2(x):
    high = x.astype(BF16)
    return high, (x - high.astype(F32)).astype(BF16)


def mm(a, b):
    return lax.dot_general(a, b, (((1,), (0,)), ((), ())), preferred_element_type=F32)


def mm3(a, b):
    return mm(a[0], b[0]) + (mm(a[0], b[1]) + mm(a[1], b[0]))


def mm2(exact, b):
    return mm(exact, b[0]) + mm(exact, b[1])


def normed_t(x_t):
    scale = lax.rsqrt(jnp.mean(x_t * x_t, axis=0, keepdims=True) + EPS)
    return x_t * scale, scale


def features_t(seed_t, normed):
    return jnp.exp(mm2(seed_t, split2(normed)) * (1.0 / SEED_DIV))


def normed_grad_t(seed, feats_t, dfeats_t, normed, scale):
    grad = mm2(seed, split2(dfeats_t * feats_t)) * (1.0 / SEED_DIV)
    return scale * (grad - normed * jnp.mean(grad * normed, axis=0, keepdims=True))


def column_to_rows(column):
    wide = jnp.transpose(jnp.broadcast_to(column, (column.shape[0], 128)))
    row = lax.broadcasted_iota(jnp.int32, (EXT, 128), 0)
    return jnp.where(row == 0, wide[:EXT, :128], wide[:EXT, 128:])


def rows_to_column(block):
    row = jnp.concatenate([block[0:1], block[1:2]], axis=1)
    return jnp.transpose(jnp.broadcast_to(row, (128, row.shape[1])))[:, :1]


def assemble(scratch, refs, member, rows):
    for distance, ref in enumerate(refs):
        place = pl.multiple_of(jnp.bitwise_xor(member, distance) * rows, rows)
        scratch[pl.ds(place, rows), :] = ref[...]


def gate_row(ext, head, members):
    logits = jnp.concatenate([ext[pl.ds(m * EXT + head, 1), :] for m in range(members)], axis=1)
    return 1.0 / (1.0 + jnp.exp(-logits))


def copy_kernel(moves_of, n_in, *refs):
    index, ins, outs, sems = refs[0], refs[1 : 1 + n_in], refs[1 + n_in : -1], refs[-1]
    copies = [
        pltpu.make_async_copy(source, target, sems.at[position])
        for position, (source, target) in enumerate(moves_of(index, ins, outs))
    ]
    for copy in copies:
        copy.start()
    for copy in copies:
        copy.wait()


def local_copies(moves_of, n_moves, index, ins, out_shapes, name):
    size = sum(math.prod(s.shape) * 4 for s in out_shapes)
    return pl.pallas_call(
        functools.partial(copy_kernel, moves_of, len(ins)),
        grid_spec=pltpu.PrefetchScalarGridSpec(
            num_scalar_prefetch=1,
            grid=(1,),
            in_specs=[pl.BlockSpec(memory_space=pl.ANY)] * len(ins),
            out_specs=[pl.BlockSpec(s.shape, lambda i, ref: (0, 0)) for s in out_shapes],
            scratch_shapes=[pltpu.SemaphoreType.DMA((n_moves,))],
        ),
        out_shape=out_shapes,
        compiler_params=pltpu.CompilerParams(vmem_limit_bytes=32 * 1024 * 1024),
        cost_estimate=pl.CostEstimate(flops=0, bytes_accessed=2 * size, transcendentals=0),
        name=name,
    )(index, *ins)


def sums_kernel(members, rows, heads, index, *refs):
    key_refs, value_refs = refs[:members], refs[members : 2 * members]
    seed_t_ref = refs[2 * members]
    keys_out, values_out, sums_out, low_edge, high_edge = refs[2 * members + 1 :]
    head = pl.program_id(0)
    member = index[0]
    tokens = members * rows
    reach = rows // 2

    @pl.when(head == 0)
    def _():
        sums_out[pl.ds(heads * 256, sums_out.shape[0] - heads * 256), :] = jnp.zeros(
            (sums_out.shape[0] - heads * 256, 128), F32
        )

    assemble(keys_out, key_refs, member, rows)
    assemble(values_out, value_refs, member, rows)
    keys, values = keys_out[...], values_out[...]
    low_edge[:reach] = keys[:reach]
    low_edge[reach:] = values[:reach]
    high_edge[:reach] = keys[tokens - reach :]
    high_edge[reach:] = values[tokens - reach :]
    normed, _ = normed_t(jnp.transpose(keys))
    feats = features_t(seed_t_ref[...], normed)
    sums_out[pl.ds(pl.multiple_of(head * 256, 256), 256), :] = mm3(split2(feats), split2(values))
    sums_out[pl.ds(pl.multiple_of(heads * 256 + head * EXT, EXT), EXT), :] = column_to_rows(
        jnp.sum(feats, axis=1, keepdims=True)
    )


def query_kernel(members, rows, heads, index, *refs):
    query_refs, grad_refs = refs[:members], refs[members : 2 * members]
    ext_refs = refs[2 * members : 3 * members]
    sums_ref, seed_ref, seed_t_ref = refs[3 * members : 3 * members + 3]
    low_out, query_out, sums_out, queries, grads, ext = refs[3 * members + 3 :]
    head = pl.program_id(0)
    member = index[0]

    @pl.when(head == 0)
    def _():
        assemble(ext, ext_refs, member, EXT)
        sums_out[pl.ds(heads * 256, sums_out.shape[0] - heads * 256), :] = jnp.zeros(
            (sums_out.shape[0] - heads * 256, 128), F32
        )

    assemble(queries, query_refs, member, rows)
    assemble(grads, grad_refs, member, rows)
    gate = gate_row(ext, head, members)
    sums = sums_ref[pl.ds(pl.multiple_of(head * 256, 256), 256), :]
    totals = rows_to_column(sums_ref[pl.ds(pl.multiple_of(heads * 256 + head * EXT, EXT), EXT), :])
    normed, scale = normed_t(jnp.transpose(queries[...]))
    feats = features_t(seed_t_ref[...], normed)
    feats_parts = split2(feats)
    inverse = 1.0 / jnp.sum(feats * totals, axis=0, keepdims=True)
    low = mm3(split2(jnp.transpose(sums)), feats_parts) * inverse
    dnum = jnp.transpose(grads[...]) * ((1.0 - gate) * inverse)
    dden = -jnp.sum(dnum * low, axis=0, keepdims=True)
    dfeats = mm3(split2(sums), split2(dnum)) + totals * dden
    low_out[...] = low
    query_out[...] = normed_grad_t(seed_ref[...], feats, dfeats, normed, scale)
    sums_out[pl.ds(pl.multiple_of(head * 256, 256), 256), :] = mm3(
        feats_parts, split2(jnp.transpose(dnum))
    )
    sums_out[pl.ds(pl.multiple_of(heads * 256 + head * EXT, EXT), EXT), :] = column_to_rows(
        jnp.sum(feats * dden, axis=1, keepdims=True)
    )


def fill_bias(bias, ext, members, rows, first, last):
    reach = rows // 2
    key_at = lax.broadcasted_iota(jnp.int32, (rows, rows), 0)
    query_at = lax.broadcasted_iota(jnp.int32, (rows, rows), 1)
    for block in range(members):
        for other in range(members):
            gap = (other - block) * rows + key_at - query_at
            allowed = jnp.abs(gap) <= reach
            if other != block:
                flag = ext[block * EXT + EXT - 1 : block * EXT + EXT, other : other + 1]
                allowed = jnp.logical_or(allowed, jnp.broadcast_to(flag, (rows, rows)) > 0.5)
            bias[other * rows : (other + 1) * rows, block * rows : (block + 1) * rows] = jnp.where(
                allowed, 0.0, NEG_FILL
            )
        allowed = jnp.zeros((rows, rows), jnp.bool_)
        if block == 0:
            allowed = (key_at < reach) & (query_at <= key_at) & (first == 0)
        if block == members - 1:
            right = (key_at >= reach) & (query_at >= key_at) & (last == 0)
            allowed = jnp.logical_or(allowed, right)
        bias[members * rows :, block * rows : (block + 1) * rows] = jnp.where(
            allowed, 0.0, NEG_FILL
        )


def sparse_kernel(members, rows, heads, index, *refs):
    query_refs, grad_refs = refs[:members], refs[members : 2 * members]
    ext_refs = refs[2 * members : 3 * members]
    keys_ref, values_ref, left_ref, right_ref, low_ref, query_low_ref = refs[
        3 * members : 3 * members + 6
    ]
    outs = refs[3 * members + 6 :]
    messages = outs[:members]
    keys_out, values_out, left_out, right_out = outs[members : members + 4]
    queries, grads, ext, bias, keys_all, values_all = outs[members + 4 :]
    head = pl.program_id(0)
    member = index[0]
    tokens = members * rows
    reach = rows // 2

    @pl.when(head == 0)
    def _():
        assemble(ext, ext_refs, member, EXT)
        fill_bias(bias, ext, members, rows, index[1], index[2])
        for message in messages:
            message[pl.ds(2 * heads * rows, EXT), :] = jnp.zeros((EXT, 128), F32)

    assemble(queries, query_refs, member, rows)
    assemble(grads, grad_refs, member, rows)
    keys_all[:tokens] = keys_ref[...]
    keys_all[tokens : tokens + reach] = left_ref[:reach]
    keys_all[tokens + reach :] = right_ref[:reach]
    values_all[:tokens] = values_ref[...]
    values_all[tokens : tokens + reach] = left_ref[reach:]
    values_all[tokens + reach :] = right_ref[reach:]

    gate = gate_row(ext, head, members)
    root = 1.0 / math.sqrt(HEAD_DIM)
    keys = split2(keys_all[...])
    values = split2(values_all[...])
    keys_t = split2(jnp.transpose(keys_all[...]))
    values_t = split2(jnp.transpose(values_all[...]))
    scaled = queries[...] * root
    scores = mm3(keys, split2(jnp.transpose(scaled))) + bias[...]
    weights = jnp.exp(scores - jnp.max(scores, axis=0, keepdims=True))
    inverse = 1.0 / jnp.sum(weights, axis=0, keepdims=True)
    weight_parts = split2(weights)
    mixed = mm3(values_t, weight_parts) * inverse
    low = low_ref[...]
    grad_t = jnp.transpose(grads[...])
    gate_grad = jnp.sum(grad_t * (mixed - low), axis=0, keepdims=True) * gate * (1.0 - gate)
    sparse_grad = grad_t * (gate * inverse)
    delta = jnp.sum(sparse_grad * mixed, axis=0, keepdims=True)
    score_grad = weights * (mm3(values, split2(sparse_grad)) - delta)
    score_parts = split2(score_grad)
    query_grad = mm3(keys_t, score_parts) * root + query_low_ref[...]
    keys_grad = mm3(score_parts, split2(scaled))
    values_grad = mm3(weight_parts, split2(jnp.transpose(sparse_grad)))
    keys_out[...] = keys_grad[:tokens]
    values_out[...] = values_grad[:tokens]
    left_out[:reach] = keys_grad[tokens : tokens + reach]
    left_out[reach:] = values_grad[tokens : tokens + reach]
    right_out[:reach] = keys_grad[tokens + reach :]
    right_out[reach:] = values_grad[tokens + reach :]
    queries[...] = jnp.transpose(gate * mixed + (1.0 - gate) * low)
    grads[...] = jnp.transpose(query_grad)
    for m in range(members):
        ext[pl.ds(m * EXT + head, 1), :] = gate_grad[:, m * rows : (m + 1) * rows]
    for distance, message in enumerate(messages):
        other = jnp.bitwise_xor(member, distance)
        place = pl.ds(pl.multiple_of(other * rows, rows), rows)
        start = pl.multiple_of(head * 2 * rows, rows)
        message[pl.ds(start, rows), :] = queries[place, :]
        message[pl.ds(start + rows, rows), :] = grads[place, :]

    @pl.when(head == heads - 1)
    def _():
        for distance, message in enumerate(messages):
            other = jnp.bitwise_xor(member, distance)
            message[pl.ds(2 * heads * rows, EXT), :] = ext[
                pl.ds(pl.multiple_of(other * EXT, EXT), EXT), :
            ]


def keys_kernel(members, rows, heads, index, *refs):
    (keys_ref, values_ref, sums_ref, keys_grad, values_grad, left_ref, right_ref, seed_ref, seed_t_ref) = refs[:9]
    messages = refs[9 : 9 + members]
    dkeys, dvalues = refs[9 + members :]
    head = pl.program_id(0)
    member = index[0]
    tokens = members * rows
    reach = rows // 2
    sums = sums_ref[pl.ds(pl.multiple_of(head * 256, 256), 256), :]
    totals = rows_to_column(sums_ref[pl.ds(pl.multiple_of(heads * 256 + head * EXT, EXT), EXT), :])
    normed, scale = normed_t(jnp.transpose(keys_ref[...]))
    feats = features_t(seed_t_ref[...], normed)
    dfeats = mm3(split2(sums), split2(jnp.transpose(values_ref[...]))) + totals
    key_low = normed_grad_t(seed_ref[...], feats, dfeats, normed, scale)
    value_low = mm3(split2(jnp.transpose(sums)), split2(feats))
    dkeys[...] = keys_grad[...] + jnp.transpose(key_low)
    dvalues[...] = values_grad[...] + jnp.transpose(value_low)
    dkeys[:reach] += left_ref[:reach]
    dvalues[:reach] += left_ref[reach:]
    dkeys[tokens - reach :] += right_ref[:reach]
    dvalues[tokens - reach :] += right_ref[reach:]
    for distance, message in enumerate(messages):
        other = jnp.bitwise_xor(member, distance)
        place = pl.ds(pl.multiple_of(other * rows, rows), rows)
        message[:rows] = dkeys[place, :]
        message[rows:] = dvalues[place, :]


def per_head_call(kernel, members, rows, heads, index, ins, outs, scratch, flops, exps, name):
    in_specs = [spec for _, spec in ins]
    size = sum(math.prod(x.shape) * 4 for x, _ in ins[-4:]) + sum(math.prod(s.shape) * 4 for s, _ in outs)
    return pl.pallas_call(
        functools.partial(kernel, members, rows, heads),
        grid_spec=pltpu.PrefetchScalarGridSpec(
            num_scalar_prefetch=1,
            grid=(heads,),
            in_specs=in_specs,
            out_specs=[spec for _, spec in outs],
            scratch_shapes=scratch,
        ),
        out_shape=[shape for shape, _ in outs],
        compiler_params=pltpu.CompilerParams(
            vmem_limit_bytes=56 * 1024 * 1024, dimension_semantics=("arbitrary",)
        ),
        cost_estimate=pl.CostEstimate(flops=flops, bytes_accessed=size, transcendentals=exps),
        name=name,
    )(index, *[x for x, _ in ins])


def swap(block, axis, distance):
    return lax.ppermute(block, axis, [(i, i ^ distance) for i in range(lax.axis_size(axis))])


def sum_over_seq(cells):
    count = lax.axis_size("seq")
    place = lax.axis_index("seq")
    core, chip = place & 1, place >> 1
    chips = count // 2
    half = cells.shape[0] // 2
    part = half // chips

    def cut(x, at, size):
        return lax.dynamic_slice_in_dim(x, at * size, size, 0)

    summed = cut(cells, core, half) + swap(cut(cells, 1 - core, half), "seq", 1)
    own = cut(summed, chip, part)
    for d in range(1, chips):
        own = own + swap(cut(summed, chip ^ d, part), "seq", 2 * d)
    gathered = jnp.zeros((half, cells.shape[1]), F32)
    gathered = lax.dynamic_update_slice_in_dim(gathered, own, chip * part, 0)
    for d in range(1, chips):
        gathered = lax.dynamic_update_slice_in_dim(
            gathered, swap(own, "seq", 2 * d), (chip ^ d) * part, 0
        )
    other = swap(gathered, "seq", 1)
    first = jnp.where(core == 0, gathered, other)
    second = jnp.where(core == 0, other, gathered)
    return jnp.concatenate([first, second], axis=0)


def to_next(block):
    count = lax.axis_size("seq")
    return lax.ppermute(block, "seq", [(i, i + 1) for i in range(count - 1)])


def to_previous(block):
    count = lax.axis_size("seq")
    return lax.ppermute(block, "seq", [(i + 1, i) for i in range(count - 1)])


def shards(
    queries,
    key_matrix,
    value_matrix,
    gate_logits,
    output_grad,
    cycle_offsets,
    block_count,
    feature_seed,
):
    rows, width = queries.shape
    members = lax.axis_size("blk")
    member = lax.axis_index("blk")
    groups = lax.axis_size("seq")
    group = lax.axis_index("seq")
    heads = gate_logits.shape[1] // members
    tokens = members * rows
    others = range(1, members)
    index = jnp.stack(
        [member, (group == 0).astype(jnp.int32), (group == groups - 1).astype(jnp.int32)]
    ).astype(jnp.int32)
    sum_rows = -(-(heads * (256 + EXT)) // (EXT * groups)) * EXT * groups

    def shape(*dims):
        return jax.ShapeDtypeStruct(dims, F32)

    def block_of(message_rows, at):
        return pl.BlockSpec((message_rows, 128), lambda h, ref: (at(h, ref), 0))

    own_spec = pl.BlockSpec((rows, 128), lambda h, ref: (0, ref[0] * heads + h))
    head_spec = pl.BlockSpec((tokens, 128), lambda h, ref: (h, 0))
    edge_spec = pl.BlockSpec((rows, 128), lambda h, ref: (h, 0))
    wide_spec = pl.BlockSpec((128, tokens), lambda h, ref: (h, 0))

    def whole(x):
        return pl.BlockSpec(x.shape, lambda h, ref: (0,) * len(x.shape))

    def packing(index, ins, outs, extra):
        moves = []
        for d, out in zip(others, outs):
            other = jnp.bitwise_xor(index[0], d)
            for a in range(2):
                for h in range(heads):
                    column = pl.multiple_of((other * heads + h) * 128, 128)
                    moves.append(
                        (ins[a].at[:, pl.ds(column, 128)], out.at[pl.ds((a * heads + h) * rows, rows), :])
                    )
            if extra:
                start = pl.multiple_of(other * EXT, EXT)
                moves.append(
                    (ins[2].at[pl.ds(start, EXT), :], out.at[pl.ds(2 * heads * rows, EXT), :])
                )
        return moves

    def unpacking(index, ins, outs):
        moves = []
        for d, message in enumerate(ins):
            other = jnp.bitwise_xor(index[0], d)
            for a in range(2):
                for h in range(heads):
                    column = pl.multiple_of((other * heads + h) * 128, 128)
                    moves.append(
                        (message.at[pl.ds((2 * h + a) * rows, rows), :], outs[a].at[:, pl.ds(column, 128)])
                    )
        return moves

    kv_sent = local_copies(
        functools.partial(packing, extra=False),
        2 * heads * (members - 1),
        index,
        [key_matrix, value_matrix],
        [shape(2 * heads * rows, 128)] * (members - 1),
        "pack_kv",
    )
    kv = [swap(block, "blk", d) for d, block in zip(others, kv_sent)]

    active = jnp.arange(cycle_offsets.shape[1], dtype=jnp.int32) < block_count[0]
    named = jnp.mod(cycle_offsets[0] + member, members)
    lanes = jnp.arange(128, dtype=jnp.int32)
    flags = jnp.any(active[:, None] & (named[:, None] == lanes[None, :]), axis=0).astype(F32)
    logits = jnp.transpose(gate_logits).reshape(members, heads, rows)
    ext = jnp.concatenate(
        [
            logits,
            jnp.zeros((members, EXT - 1 - heads, rows), F32),
            jnp.broadcast_to(flags[None, None, :], (members, 1, 128)),
        ],
        axis=1,
    ).reshape(members * EXT, 128)
    qd_sent = local_copies(
        functools.partial(packing, extra=True),
        (2 * heads + 1) * (members - 1),
        index,
        [queries, output_grad, ext],
        [shape(2 * heads * rows + EXT, 128)] * (members - 1),
        "pack_qd",
    )
    kv, qd_sent = lax.optimization_barrier((kv, qd_sent))
    qd = [swap(block, "blk", d) for d, block in zip(others, qd_sent)]

    seed = feature_seed.astype(BF16)
    seed_t = jnp.transpose(feature_seed).astype(BF16)
    unit = 2 * tokens * 128 * 256
    first_block = block_of(rows, lambda h, ref: h)
    second_block = block_of(rows, lambda h, ref: heads + h)
    keys_full, values_full, sums, low_edge, high_edge = per_head_call(
        sums_kernel,
        members,
        rows,
        heads,
        index,
        [(key_matrix, own_spec)]
        + [(x, first_block) for x in kv]
        + [(value_matrix, own_spec)]
        + [(x, second_block) for x in kv]
        + [(seed_t, whole(seed_t))],
        [
            (shape(heads * tokens, 128), head_spec),
            (shape(heads * tokens, 128), head_spec),
            (shape(sum_rows, 128), whole(shape(sum_rows, 128))),
            (shape(heads * rows, 128), edge_spec),
            (shape(heads * rows, 128), edge_spec),
        ],
        [],
        5 * unit * heads,
        heads * tokens * 256,
        "key_sums",
    )
    right_halo = to_previous(low_edge)
    left_halo = to_next(high_edge)
    sums = sum_over_seq(sums)

    ext_block = block_of(EXT, lambda h, ref: 2 * heads * rows // EXT)
    query_side = (
        [(queries, own_spec)]
        + [(x, first_block) for x in qd]
        + [(output_grad, own_spec)]
        + [(x, second_block) for x in qd]
        + [(ext, block_of(EXT, lambda h, ref: ref[0]))]
        + [(x, ext_block) for x in qd]
    )
    row_scratch = [
        pltpu.VMEM((tokens, 128), F32),
        pltpu.VMEM((tokens, 128), F32),
        pltpu.VMEM((members * EXT, 128), F32),
    ]
    low, query_low, sums_grad = per_head_call(
        query_kernel,
        members,
        rows,
        heads,
        index,
        query_side + [(sums, whole(sums)), (seed, whole(seed)), (seed_t, whole(seed_t))],
        [
            (shape(heads * 128, tokens), wide_spec),
            (shape(heads * 128, tokens), wide_spec),
            (shape(sum_rows, 128), whole(shape(sum_rows, 128))),
        ],
        row_scratch,
        13 * unit * heads,
        heads * tokens * 256,
        "query_low_rank",
    )
    sums_grad = sum_over_seq(sums_grad)

    message = shape(2 * heads * rows + EXT, 128)
    sparse_outs = per_head_call(
        sparse_kernel,
        members,
        rows,
        heads,
        index,
        query_side
        + [
            (keys_full, head_spec),
            (values_full, head_spec),
            (left_halo, edge_spec),
            (right_halo, edge_spec),
            (low, wide_spec),
            (query_low, wide_spec),
        ],
        [(message, whole(message))] * members
        + [
            (shape(heads * tokens, 128), head_spec),
            (shape(heads * tokens, 128), head_spec),
            (shape(heads * rows, 128), edge_spec),
            (shape(heads * rows, 128), edge_spec),
        ],
        row_scratch
        + [
            pltpu.VMEM((tokens + rows, tokens), F32),
            pltpu.VMEM((tokens + rows, 128), F32),
            pltpu.VMEM((tokens + rows, 128), F32),
        ],
        36 * tokens * (tokens + rows) * 128 * heads,
        heads * tokens * (tokens + rows),
        "sparse",
    )
    od_sent = sparse_outs[:members]
    keys_sparse, values_sparse, left_grad, right_grad = sparse_outs[members:]
    od = [od_sent[0]] + [swap(block, "blk", d) for d, block in zip(others, od_sent[1:])]
    back_right = to_previous(left_grad)
    back_left = to_next(right_grad)

    dkv_sent = per_head_call(
        keys_kernel,
        members,
        rows,
        heads,
        index,
        [
            (keys_full, head_spec),
            (values_full, head_spec),
            (sums_grad, whole(sums_grad)),
            (keys_sparse, head_spec),
            (values_sparse, head_spec),
            (back_left, edge_spec),
            (back_right, edge_spec),
            (seed, whole(seed)),
            (seed_t, whole(seed_t)),
        ],
        [(shape(2 * heads * rows, 128), pl.BlockSpec((2 * rows, 128), lambda h, ref: (h, 0)))]
        * members,
        [pltpu.VMEM((tokens, 128), F32), pltpu.VMEM((tokens, 128), F32)],
        10 * unit * heads,
        heads * tokens * 256,
        "key_low_rank",
    )
    dkv = [dkv_sent[0]] + [swap(block, "blk", d) for d, block in zip(others, dkv_sent[1:])]

    attended, query_grad = local_copies(
        unpacking, 2 * heads * members, index, od, [shape(rows, width)] * 2, "unpack_od"
    )
    ext_back = jnp.zeros((members, EXT, 128), F32)
    for d, block in enumerate(od):
        ext_back = lax.dynamic_update_slice_in_dim(
            ext_back, block[None, 2 * heads * rows :, :], member ^ d, 0
        )
    gate_grad = jnp.transpose(ext_back[:, :heads, :].reshape(members * heads, rows))
    key_grad, value_grad = local_copies(
        unpacking, 2 * heads * members, index, dkv, [shape(rows, width)] * 2, "unpack_kv"
    )
    return (attended, query_grad, key_grad, value_grad, gate_grad)


def solution(mesh):
    row_spec = P(("seq", "blk"), None)
    return jax.shard_map(
        shards,
        mesh=mesh,
        in_specs=(row_spec,) * 6 + (P(("seq", "blk")), P()),
        out_specs=(row_spec,) * 5,
        check_vma=False,
    )
```

```python
import functools
import math

import jax
import jax.numpy as jnp
from jax import lax
from jax.experimental import pallas as pl
from jax.experimental.pallas import tpu as pltpu
from jax.sharding import PartitionSpec as P

HEAD_DIM = 128
EXT = 8
NEG_FILL = -1e30
SEED_DIV = 13.0
EPS = 1e-06
F32 = jnp.float32
BF16 = jnp.bfloat16


def split2(x):
    high = x.astype(BF16)
    return high, (x - high.astype(F32)).astype(BF16)


def mm(a, b):
    return lax.dot_general(a, b, (((1,), (0,)), ((), ())), preferred_element_type=F32)


def mm3(a, b):
    return mm(a[0], b[0]) + (mm(a[0], b[1]) + mm(a[1], b[0]))


def split3(x):
    high = x.astype(BF16)
    rest = x - high.astype(F32)
    middle = rest.astype(BF16)
    return high, middle, (rest - middle.astype(F32)).astype(BF16)


def mm_exact(exact, b):
    total = mm(exact, b[-1])
    for part in b[-2::-1]:
        total = mm(exact, part) + total
    return total


def mm6(a, b):
    left = jnp.concatenate([a[0], a[1], a[2], a[0], a[1], a[0]], axis=1)
    right = jnp.concatenate([b[0], b[0], b[0], b[1], b[1], b[2]], axis=0)
    return mm(left, right)


def normed_t(x_t):
    scale = lax.rsqrt(jnp.mean(x_t * x_t, axis=0, keepdims=True) + EPS)
    return x_t * scale, scale


def features_t(seed_t, normed):
    return jnp.exp(mm_exact(seed_t, split3(normed)) * (1.0 / SEED_DIV))


def normed_grad_t(seed, feats_t, dfeats_t, normed, scale):
    grad = mm_exact(seed, split2(dfeats_t * feats_t)) * (1.0 / SEED_DIV)
    return scale * (grad - normed * jnp.mean(grad * normed, axis=0, keepdims=True))


def column_to_rows(column):
    wide = jnp.transpose(jnp.broadcast_to(column, (column.shape[0], 128)))
    row = lax.broadcasted_iota(jnp.int32, (EXT, 128), 0)
    return jnp.where(row == 0, wide[:EXT, :128], wide[:EXT, 128:])


def rows_to_column(block):
    row = jnp.concatenate([block[0:1], block[1:2]], axis=1)
    return jnp.transpose(jnp.broadcast_to(row, (128, row.shape[1])))[:, :1]


def assemble(scratch, refs, member, rows):
    for distance, ref in enumerate(refs):
        place = pl.multiple_of(jnp.bitwise_xor(member, distance) * rows, rows)
        scratch[pl.ds(place, rows), :] = ref[...]


def assemble_sums(scratch, mine_ref, other_ref, index, chips):
    half = mine_ref.shape[0]
    part = half // chips
    for position, ref in ((index[3], mine_ref), (1 - index[3], other_ref)):
        for distance in range(chips):
            place = position * half + jnp.bitwise_xor(index[4], distance) * part
            scratch[pl.ds(pl.multiple_of(place, EXT), part), :] = ref[
                distance * part : (distance + 1) * part
            ]


def split_sums(scratch, mine_out, other_out, index):
    half = mine_out.shape[0]
    mine_out[...] = scratch[pl.ds(pl.multiple_of(index[3] * half, EXT), half), :]
    other_out[...] = scratch[pl.ds(pl.multiple_of((1 - index[3]) * half, EXT), half), :]


def cut_kernel(index, mine_ref, got_ref, *refs):
    parts, total = refs[:-1], refs[-1]
    total[...] = mine_ref[...] + got_ref[...]
    size = parts[0].shape[0]
    for distance, part in enumerate(parts):
        place = jnp.bitwise_xor(index[4], distance) * size
        part[...] = total[pl.ds(pl.multiple_of(place, EXT), size), :]


def gate_row(ext, head, members):
    logits = jnp.concatenate([ext[pl.ds(m * EXT + head, 1), :] for m in range(members)], axis=1)
    return 1.0 / (1.0 + jnp.exp(-logits))


def copy_kernel(moves_of, n_in, *refs):
    index, ins, outs, sems = refs[0], refs[1 : 1 + n_in], refs[1 + n_in : -1], refs[-1]
    copies = [
        pltpu.make_async_copy(source, target, sems.at[position])
        for position, (source, target) in enumerate(moves_of(index, ins, outs))
    ]
    for copy in copies:
        copy.start()
    for copy in copies:
        copy.wait()


def local_copies(moves_of, n_moves, index, ins, out_shapes, name):
    size = sum(math.prod(s.shape) * 4 for s in out_shapes)
    return pl.pallas_call(
        functools.partial(copy_kernel, moves_of, len(ins)),
        grid_spec=pltpu.PrefetchScalarGridSpec(
            num_scalar_prefetch=1,
            grid=(1,),
            in_specs=[pl.BlockSpec(memory_space=pl.ANY)] * len(ins),
            out_specs=[pl.BlockSpec(s.shape, lambda i, ref: (0, 0)) for s in out_shapes],
            scratch_shapes=[pltpu.SemaphoreType.DMA((n_moves,))],
        ),
        out_shape=out_shapes,
        compiler_params=pltpu.CompilerParams(vmem_limit_bytes=32 * 1024 * 1024),
        cost_estimate=pl.CostEstimate(flops=0, bytes_accessed=2 * size, transcendentals=0),
        name=name,
    )(index, *ins)


def sums_kernel(dims, index, *refs):
    members, rows, heads, _, _, _ = dims
    key_refs, value_refs = refs[:members], refs[members : 2 * members]
    seed_t_ref = refs[2 * members]
    keys_out, values_out, mine_out, other_out, low_edge, high_edge, sums_out = refs[
        2 * members + 1 :
    ]
    head = pl.program_id(0)
    member = index[0]
    tokens = members * rows
    reach = rows // 2

    @pl.when(head == 0)
    def _():
        sums_out[pl.ds(heads * 256, sums_out.shape[0] - heads * 256), :] = jnp.zeros(
            (sums_out.shape[0] - heads * 256, 128), F32
        )

    assemble(keys_out, key_refs, member, rows)
    assemble(values_out, value_refs, member, rows)
    keys, values = keys_out[...], values_out[...]
    low_edge[:reach] = keys[:reach]
    low_edge[reach:] = values[:reach]
    high_edge[:reach] = keys[tokens - reach :]
    high_edge[reach:] = values[tokens - reach :]
    normed, _ = normed_t(jnp.transpose(keys))
    feats = features_t(seed_t_ref[...], normed)
    sums_out[pl.ds(pl.multiple_of(head * 256, 256), 256), :] = mm3(split2(feats), split2(values))
    sums_out[pl.ds(pl.multiple_of(heads * 256 + head * EXT, EXT), EXT), :] = column_to_rows(
        jnp.sum(feats, axis=1, keepdims=True)
    )

    @pl.when(head == heads - 1)
    def _():
        split_sums(sums_out, mine_out, other_out, index)


def query_kernel(dims, index, *refs):
    members, rows, heads, chips, _, _ = dims
    query_refs, grad_refs = refs[:members], refs[members : 2 * members]
    ext_refs = refs[2 * members : 3 * members]
    mine_ref, other_ref, seed_ref, seed_t_ref = refs[3 * members : 3 * members + 4]
    low_out, query_out, mine_out, other_out, queries, grads, ext, sums_ref, sums_out = refs[
        3 * members + 4 :
    ]
    head = pl.program_id(0)
    member = index[0]

    @pl.when(head == 0)
    def _():
        assemble(ext, ext_refs, member, EXT)
        assemble_sums(sums_ref, mine_ref, other_ref, index, chips)
        sums_out[pl.ds(heads * 256, sums_out.shape[0] - heads * 256), :] = jnp.zeros(
            (sums_out.shape[0] - heads * 256, 128), F32
        )

    assemble(queries, query_refs, member, rows)
    assemble(grads, grad_refs, member, rows)
    gate = gate_row(ext, head, members)
    sums = sums_ref[pl.ds(pl.multiple_of(head * 256, 256), 256), :]
    totals = rows_to_column(sums_ref[pl.ds(pl.multiple_of(heads * 256 + head * EXT, EXT), EXT), :])
    normed, scale = normed_t(jnp.transpose(queries[...]))
    feats = features_t(seed_t_ref[...], normed)
    feats_parts = split2(feats)
    inverse = 1.0 / jnp.sum(feats * totals, axis=0, keepdims=True)
    low = mm3(split2(jnp.transpose(sums)), feats_parts) * inverse
    dnum = jnp.transpose(grads[...]) * ((1.0 - gate) * inverse)
    dden = -jnp.sum(dnum * low, axis=0, keepdims=True)
    dfeats = mm3(split2(sums), split2(dnum)) + totals * dden
    low_out[...] = low
    query_out[...] = normed_grad_t(seed_ref[...], feats, dfeats, normed, scale)
    sums_out[pl.ds(pl.multiple_of(head * 256, 256), 256), :] = mm3(
        feats_parts, split2(jnp.transpose(dnum))
    )
    sums_out[pl.ds(pl.multiple_of(heads * 256 + head * EXT, EXT), EXT), :] = column_to_rows(
        jnp.sum(feats * dden, axis=1, keepdims=True)
    )

    @pl.when(head == heads - 1)
    def _():
        split_sums(sums_out, mine_out, other_out, index)


def fill_bias(bias, ext, members, rows, first, last):
    reach = rows // 2
    key_at = lax.broadcasted_iota(jnp.int32, (rows, rows), 0)
    query_at = lax.broadcasted_iota(jnp.int32, (rows, rows), 1)
    for block in range(members):
        for other in range(members):
            gap = (other - block) * rows + key_at - query_at
            allowed = jnp.abs(gap) <= reach
            if other != block:
                flag = ext[block * EXT + EXT - 1 : block * EXT + EXT, other : other + 1]
                allowed = jnp.logical_or(allowed, jnp.broadcast_to(flag, (rows, rows)) > 0.5)
            bias[other * rows : (other + 1) * rows, block * rows : (block + 1) * rows] = jnp.where(
                allowed, 0.0, NEG_FILL
            )
        allowed = jnp.zeros((rows, rows), jnp.bool_)
        if block == 0:
            allowed = (key_at < reach) & (query_at <= key_at) & (first == 0)
        if block == members - 1:
            right = (key_at >= reach) & (query_at >= key_at) & (last == 0)
            allowed = jnp.logical_or(allowed, right)
        bias[members * rows :, block * rows : (block + 1) * rows] = jnp.where(
            allowed, 0.0, NEG_FILL
        )


def sparse_kernel(dims, index, *refs):
    members, rows, heads, _, start, _ = dims
    query_refs, grad_refs = refs[:members], refs[members : 2 * members]
    ext_refs = refs[2 * members : 3 * members]
    keys_ref, values_ref, left_ref, right_ref, low_ref, query_low_ref = refs[
        3 * members : 3 * members + 6
    ]
    outs = refs[3 * members + 6 :]
    messages = outs[:members]
    keys_out, values_out, left_out, right_out = outs[members : members + 4]
    queries, grads, ext, bias, keys_all, values_all = outs[members + 4 :]
    step = pl.program_id(0)
    head = step + start
    member = index[0]
    tokens = members * rows
    reach = rows // 2

    @pl.when(step == 0)
    def _():
        assemble(ext, ext_refs, member, EXT)
        fill_bias(bias, ext, members, rows, index[1], index[2])
        for message in messages:
            message[pl.ds(2 * heads * rows, EXT), :] = jnp.zeros((EXT, 128), F32)

    assemble(queries, query_refs, member, rows)
    assemble(grads, grad_refs, member, rows)
    keys_all[:tokens] = keys_ref[...]
    keys_all[tokens : tokens + reach] = left_ref[:reach]
    keys_all[tokens + reach :] = right_ref[:reach]
    values_all[:tokens] = values_ref[...]
    values_all[tokens : tokens + reach] = left_ref[reach:]
    values_all[tokens + reach :] = right_ref[reach:]

    gate = gate_row(ext, head, members)
    root = 1.0 / math.sqrt(HEAD_DIM)
    values = split2(values_all[...])
    keys_t = split2(jnp.transpose(keys_all[...]))
    values_t = split2(jnp.transpose(values_all[...]))
    scaled = queries[...] * root
    scores = mm6(split3(keys_all[...]), split3(jnp.transpose(scaled))) + bias[...]
    weights = jnp.exp(scores - jnp.max(scores, axis=0, keepdims=True))
    inverse = 1.0 / jnp.sum(weights, axis=0, keepdims=True)
    weight_parts = split2(weights)
    mixed = mm3(values_t, weight_parts) * inverse
    low = low_ref[...]
    grad_t = jnp.transpose(grads[...])
    gate_grad = jnp.sum(grad_t * (mixed - low), axis=0, keepdims=True) * gate * (1.0 - gate)
    sparse_grad = grad_t * (gate * inverse)
    delta = jnp.sum(sparse_grad * mixed, axis=0, keepdims=True)
    score_grad = weights * (mm3(values, split2(sparse_grad)) - delta)
    score_parts = split2(score_grad)
    query_grad = mm3(keys_t, score_parts) * root + query_low_ref[...]
    keys_grad = mm3(score_parts, split2(scaled))
    values_grad = mm3(weight_parts, split2(jnp.transpose(sparse_grad)))
    keys_out[...] = keys_grad[:tokens]
    values_out[...] = values_grad[:tokens]
    left_out[:reach] = keys_grad[tokens : tokens + reach]
    left_out[reach:] = values_grad[tokens : tokens + reach]
    right_out[:reach] = keys_grad[tokens + reach :]
    right_out[reach:] = values_grad[tokens + reach :]
    queries[...] = jnp.transpose(gate * mixed + (1.0 - gate) * low)
    grads[...] = jnp.transpose(query_grad)
    for m in range(members):
        ext[pl.ds(m * EXT + head, 1), :] = gate_grad[:, m * rows : (m + 1) * rows]
    for distance, message in enumerate(messages):
        other = jnp.bitwise_xor(member, distance)
        place = pl.ds(pl.multiple_of(other * rows, rows), rows)
        at = pl.multiple_of(step * 2 * rows, rows)
        message[pl.ds(at, rows), :] = queries[place, :]
        message[pl.ds(at + rows, rows), :] = grads[place, :]

    @pl.when(step == heads - 1)
    def _():
        for distance, message in enumerate(messages):
            other = jnp.bitwise_xor(member, distance)
            message[pl.ds(2 * heads * rows, EXT), :] = ext[
                pl.ds(pl.multiple_of(other * EXT, EXT), EXT), :
            ]


def keys_kernel(dims, index, *refs):
    members, rows, _, chips, start, heads = dims
    keys_ref, values_ref, mine_ref, other_ref, keys_grad, values_grad = refs[:6]
    left_ref, right_ref, seed_ref, seed_t_ref = refs[6:10]
    messages = refs[10 : 10 + members]
    dkeys, dvalues, sums_ref = refs[10 + members :]
    step = pl.program_id(0)
    head = step + start
    member = index[0]
    tokens = members * rows
    reach = rows // 2

    @pl.when(step == 0)
    def _():
        assemble_sums(sums_ref, mine_ref, other_ref, index, chips)

    sums = sums_ref[pl.ds(pl.multiple_of(head * 256, 256), 256), :]
    totals = rows_to_column(sums_ref[pl.ds(pl.multiple_of(heads * 256 + head * EXT, EXT), EXT), :])
    normed, scale = normed_t(jnp.transpose(keys_ref[...]))
    feats = features_t(seed_t_ref[...], normed)
    dfeats = mm3(split2(sums), split2(jnp.transpose(values_ref[...]))) + totals
    key_low = normed_grad_t(seed_ref[...], feats, dfeats, normed, scale)
    value_low = mm3(split2(jnp.transpose(sums)), split2(feats))
    dkeys[...] = keys_grad[...] + jnp.transpose(key_low)
    dvalues[...] = values_grad[...] + jnp.transpose(value_low)
    dkeys[:reach] += left_ref[:reach]
    dvalues[:reach] += left_ref[reach:]
    dkeys[tokens - reach :] += right_ref[:reach]
    dvalues[tokens - reach :] += right_ref[reach:]
    for distance, message in enumerate(messages):
        other = jnp.bitwise_xor(member, distance)
        place = pl.ds(pl.multiple_of(other * rows, rows), rows)
        message[:rows] = dkeys[place, :]
        message[rows:] = dvalues[place, :]


def per_head_call(kernel, dims, index, ins, outs, scratch, flops, exps, name):
    heads = dims[2]
    size = sum(math.prod(s.shape) * 4 for s, _ in outs)
    return pl.pallas_call(
        functools.partial(kernel, dims),
        grid_spec=pltpu.PrefetchScalarGridSpec(
            num_scalar_prefetch=1,
            grid=(heads,),
            in_specs=[spec for _, spec in ins],
            out_specs=[spec for _, spec in outs],
            scratch_shapes=scratch,
        ),
        out_shape=[shape for shape, _ in outs],
        compiler_params=pltpu.CompilerParams(
            vmem_limit_bytes=56 * 1024 * 1024, dimension_semantics=("arbitrary",)
        ),
        cost_estimate=pl.CostEstimate(
            flops=flops * heads, bytes_accessed=2 * size, transcendentals=exps * heads
        ),
        name=name,
    )(index, *[x for x, _ in ins])


def swap(block, axis, distance):
    return lax.ppermute(block, axis, [(i, i ^ distance) for i in range(lax.axis_size(axis))])


def cut_sums(index, mine, got):
    chips = lax.axis_size("seq") // 2
    part = jax.ShapeDtypeStruct((mine.shape[0] // chips, 128), F32)
    return pl.pallas_call(
        cut_kernel,
        grid_spec=pltpu.PrefetchScalarGridSpec(
            num_scalar_prefetch=1,
            grid=(1,),
            in_specs=[pl.BlockSpec(mine.shape, lambda i, ref: (0, 0))] * 2,
            out_specs=[pl.BlockSpec(part.shape, lambda i, ref: (0, 0))] * chips,
            scratch_shapes=[pltpu.VMEM(mine.shape, F32)],
        ),
        out_shape=[part] * chips,
        cost_estimate=pl.CostEstimate(
            flops=mine.size, bytes_accessed=12 * mine.size, transcendentals=0
        ),
        name="cut_sums",
    )(index, mine, got)


def reduce_parts(parts):
    own = parts[0]
    for d, part in enumerate(parts[1:], 1):
        own = own + swap(part, "seq", 2 * d)
    return own


def gather_parts(own):
    chips = lax.axis_size("seq") // 2
    return jnp.concatenate([own] + [swap(own, "seq", 2 * d) for d in range(1, chips)], axis=0)


def after(value, *others):
    return lax.optimization_barrier((value, *others))[0]


def to_next(block):
    count = lax.axis_size("seq")
    return lax.ppermute(block, "seq", [(i, i + 1) for i in range(count - 1)])


def to_previous(block):
    count = lax.axis_size("seq")
    return lax.ppermute(block, "seq", [(i + 1, i) for i in range(count - 1)])


def shards(
    queries,
    key_matrix,
    value_matrix,
    gate_logits,
    output_grad,
    cycle_offsets,
    block_count,
    feature_seed,
):
    rows, width = queries.shape
    members = lax.axis_size("blk")
    member = lax.axis_index("blk")
    groups = lax.axis_size("seq")
    group = lax.axis_index("seq")
    chips = groups // 2
    heads = gate_logits.shape[1] // members
    tokens = members * rows
    others = range(1, members)
    index = jnp.stack(
        [
            member,
            (group == 0).astype(jnp.int32),
            (group == groups - 1).astype(jnp.int32),
            group & 1,
            group >> 1,
        ]
    ).astype(jnp.int32)
    sum_rows = -(-(heads * (256 + EXT)) // (EXT * groups)) * EXT * groups
    chunks = [(0, heads // 2), (heads // 2, heads - heads // 2)]
    dims = (members, rows, heads, chips, 0, heads)

    def shape(*sizes):
        return jax.ShapeDtypeStruct(sizes, F32)

    def block_of(message_rows, at):
        return pl.BlockSpec((message_rows, 128), lambda h, ref: (at(h, ref), 0))

    def per_head(block, start=0):
        return pl.BlockSpec(block, lambda h, ref: (h + start, 0))

    def whole(x):
        return pl.BlockSpec(x.shape, lambda h, ref: (0,) * len(x.shape))

    def packing(index, ins, outs, extra):
        moves = []
        for d, out in zip(others, outs):
            other = jnp.bitwise_xor(index[0], d)
            for a in range(2):
                for h in range(heads):
                    column = pl.multiple_of((other * heads + h) * 128, 128)
                    moves.append(
                        (
                            ins[a].at[:, pl.ds(column, 128)],
                            out.at[pl.ds((a * heads + h) * rows, rows), :],
                        )
                    )
            if extra:
                start = pl.multiple_of(other * EXT, EXT)
                moves.append(
                    (ins[2].at[pl.ds(start, EXT), :], out.at[pl.ds(2 * heads * rows, EXT), :])
                )
        return moves

    def unpacking(index, ins, outs):
        moves = []
        for chunk, (start, count) in enumerate(chunks):
            for d in range(members):
                other = jnp.bitwise_xor(index[0], d)
                message = ins[chunk * members + d]
                for a in range(2):
                    for h in range(count):
                        column = pl.multiple_of((other * heads + start + h) * 128, 128)
                        moves.append(
                            (
                                message.at[pl.ds((2 * h + a) * rows, rows), :],
                                outs[a].at[:, pl.ds(column, 128)],
                            )
                        )
        return moves

    kv_sent = local_copies(
        functools.partial(packing, extra=False),
        2 * heads * (members - 1),
        index,
        [key_matrix, value_matrix],
        [shape(2 * heads * rows, 128)] * (members - 1),
        "pack_kv",
    )
    kv = [swap(block, "blk", d) for d, block in zip(others, kv_sent)]

    active = jnp.arange(cycle_offsets.shape[1], dtype=jnp.int32) < block_count[0]
    named = jnp.mod(cycle_offsets[0] + member, members)
    lanes = jnp.arange(128, dtype=jnp.int32)
    flags = jnp.any(active[:, None] & (named[:, None] == lanes[None, :]), axis=0).astype(F32)
    logits = jnp.transpose(gate_logits).reshape(members, heads, rows)
    ext = jnp.concatenate(
        [
            logits,
            jnp.zeros((members, EXT - 1 - heads, rows), F32),
            jnp.broadcast_to(flags[None, None, :], (members, 1, 128)),
        ],
        axis=1,
    ).reshape(members * EXT, 128)
    qd_sent = local_copies(
        functools.partial(packing, extra=True),
        (2 * heads + 1) * (members - 1),
        index,
        [queries, output_grad, ext],
        [shape(2 * heads * rows + EXT, 128)] * (members - 1),
        "pack_qd",
    )
    kv, qd_sent = lax.optimization_barrier((kv, qd_sent))
    qd = [swap(block, "blk", d) for d, block in zip(others, qd_sent)]

    seed = feature_seed.astype(BF16)
    seed_t = jnp.transpose(feature_seed).astype(BF16)
    unit = 2 * tokens * 128 * 256
    exps = tokens * 256
    half = shape(sum_rows // 2, 128)
    all_sums = pltpu.VMEM((sum_rows, 128), F32)
    own_spec = pl.BlockSpec((rows, 128), lambda h, ref: (0, ref[0] * heads + h))
    keys_full, values_full, sums, sums_other, low_edge, high_edge = per_head_call(
        sums_kernel,
        dims,
        index,
        [(key_matrix, own_spec)]
        + [(x, per_head((rows, 128))) for x in kv]
        + [(value_matrix, own_spec)]
        + [(x, per_head((rows, 128), heads)) for x in kv]
        + [(seed_t, whole(seed_t))],
        [
            (shape(heads * tokens, 128), per_head((tokens, 128))),
            (shape(heads * tokens, 128), per_head((tokens, 128))),
            (half, whole(half)),
            (half, whole(half)),
            (shape(heads * rows, 128), per_head((rows, 128))),
            (shape(heads * rows, 128), per_head((rows, 128))),
        ],
        [all_sums],
        6 * unit,
        exps,
        "key_sums",
    )
    right_halo = to_previous(low_edge)
    left_halo = to_next(high_edge)
    sums = reduce_parts(cut_sums(index, sums, swap(sums_other, "seq", 1)))
    sums, *qd[:2] = lax.optimization_barrier((sums, *qd[:2]))
    sums = gather_parts(sums)
    sums_other = swap(sums, "seq", 1)

    ext_block = block_of(EXT, lambda h, ref: 2 * heads * rows // EXT)

    def query_side(start):
        own = pl.BlockSpec((rows, 128), lambda h, ref: (0, ref[0] * heads + start + h))
        return (
            [(queries, own)]
            + [(x, per_head((rows, 128), start)) for x in qd]
            + [(output_grad, own)]
            + [(x, per_head((rows, 128), heads + start)) for x in qd]
            + [(ext, block_of(EXT, lambda h, ref: ref[0]))]
            + [(x, ext_block) for x in qd]
        )

    row_scratch = [
        pltpu.VMEM((tokens, 128), F32),
        pltpu.VMEM((tokens, 128), F32),
        pltpu.VMEM((members * EXT, 128), F32),
    ]
    low, query_low, sums_grad, grad_other = per_head_call(
        query_kernel,
        dims,
        index,
        query_side(0)
        + [
            (sums, whole(sums)),
            (sums_other, whole(sums_other)),
            (seed, whole(seed)),
            (seed_t, whole(seed_t)),
        ],
        [
            (shape(heads * 128, tokens), per_head((128, tokens))),
            (shape(heads * 128, tokens), per_head((128, tokens))),
            (half, whole(half)),
            (half, whole(half)),
        ],
        row_scratch + [all_sums, all_sums],
        14 * unit,
        exps,
        "query_low_rank",
    )

    def sparse(chunk, low, query_low):
        start, count = chunks[chunk]
        message = shape(2 * count * rows + EXT, 128)
        outs = per_head_call(
            sparse_kernel,
            (members, rows, count, chips, start, heads),
            index,
            query_side(start)
            + [
                (keys_full, per_head((tokens, 128), start)),
                (values_full, per_head((tokens, 128), start)),
                (left_halo, per_head((rows, 128), start)),
                (right_halo, per_head((rows, 128), start)),
                (low, per_head((128, tokens), start)),
                (query_low, per_head((128, tokens), start)),
            ],
            [(message, whole(message))] * members
            + [(shape(count * tokens, 128), per_head((tokens, 128)))] * 2
            + [(shape(count * rows, 128), per_head((rows, 128)))] * 2,
            row_scratch
            + [
                pltpu.VMEM((tokens + rows, tokens), F32),
                pltpu.VMEM((tokens + rows, 128), F32),
                pltpu.VMEM((tokens + rows, 128), F32),
            ],
            42 * tokens * (tokens + rows) * 128,
            tokens * (tokens + rows),
            "sparse",
        )
        return outs[:members], outs[members:]

    def key_side(chunk, parts, sums, sums_other):
        start, count = chunks[chunk]
        keys_sparse, values_sparse, left_grad, right_grad = parts
        back_right = to_previous(left_grad)
        back_left = to_next(right_grad)
        message = shape(2 * count * rows, 128)
        return per_head_call(
            keys_kernel,
            (members, rows, count, chips, start, heads),
            index,
            [
                (keys_full, per_head((tokens, 128), start)),
                (values_full, per_head((tokens, 128), start)),
                (sums, whole(sums)),
                (sums_other, whole(sums_other)),
                (keys_sparse, per_head((tokens, 128))),
                (values_sparse, per_head((tokens, 128))),
                (back_left, per_head((rows, 128))),
                (back_right, per_head((rows, 128))),
                (seed, whole(seed)),
                (seed_t, whole(seed_t)),
            ],
            [(message, per_head((2 * rows, 128)))] * members,
            [pltpu.VMEM((tokens, 128), F32), pltpu.VMEM((tokens, 128), F32), all_sums],
            13 * unit,
            exps,
            "key_low_rank",
        )

    def back(messages):
        return [messages[0]] + [swap(block, "blk", d) for d, block in zip(others, messages[1:])]

    parts = cut_sums(index, sums_grad, swap(grad_other, "seq", 1))
    low, query_low, *parts = lax.optimization_barrier((low, query_low, *parts))
    od_first, keys_first = sparse(0, low, query_low)
    own = reduce_parts(parts)
    low, query_low, own, *od_first = lax.optimization_barrier((low, query_low, own, *od_first))
    od_first = back(od_first)
    od_second, keys_second = sparse(1, low, query_low)
    sums = gather_parts(own)
    sums, *od_second = lax.optimization_barrier((sums, *od_second))
    sums_other = swap(sums, "seq", 1)
    od_second = back(od_second)
    dkv_first = back(key_side(0, keys_first, sums, sums_other))
    dkv_second = back(key_side(1, keys_second, sums, sums_other))

    od = od_first + od_second
    n_moves = 2 * heads * members
    attended, query_grad = local_copies(
        unpacking, n_moves, index, od, [shape(rows, width)] * 2, "unpack_od"
    )
    gate_parts = []
    for chunk, (start, count) in enumerate(chunks):
        rows_back = jnp.zeros((members, EXT, 128), F32)
        for d in range(members):
            block = od[chunk * members + d]
            rows_back = lax.dynamic_update_slice_in_dim(
                rows_back, block[None, 2 * count * rows :, :], member ^ d, 0
            )
        gate_parts.append(rows_back[:, start : start + count, :])
    gate_grad = jnp.concatenate(gate_parts, axis=1).reshape(members * heads, rows)
    key_grad, value_grad = local_copies(
        unpacking,
        n_moves,
        index,
        dkv_first + dkv_second,
        [shape(rows, width)] * 2,
        "unpack_kv",
    )
    return (attended, query_grad, key_grad, value_grad, jnp.transpose(gate_grad))


def solution(mesh):
    row_spec = P(("seq", "blk"), None)
    return jax.shard_map(
        shards,
        mesh=mesh,
        in_specs=(row_spec,) * 6 + (P(("seq", "blk")), P()),
        out_specs=(row_spec,) * 5,
        check_vma=False,
    )
```

```python
import functools
import math

import jax
import jax.numpy as jnp
from jax import lax
from jax.experimental import pallas as pl
from jax.experimental.pallas import tpu as pltpu
from jax.sharding import PartitionSpec as P

HEAD_DIM = 128
EXT = 8
NEG_FILL = -1e30
SEED_DIV = 13.0
EPS = 1e-06
F32 = jnp.float32
BF16 = jnp.bfloat16


def split2(x):
    high = x.astype(BF16)
    return high, (x - high.astype(F32)).astype(BF16)


def mm(a, b):
    return lax.dot_general(a, b, (((1,), (0,)), ((), ())), preferred_element_type=F32)


def mm3_deep(a, b):
    return mm(
        jnp.concatenate([a[0], a[1], a[0]], axis=1), jnp.concatenate([b[0], b[0], b[1]], axis=0)
    )


def mm3_tall(a, b):
    rows = a[0].shape[0]
    both = mm(jnp.concatenate(a, axis=0), b[0])
    return both[:rows] + (both[rows:] + mm(a[0], b[1]))


def mm3_wide(a, b):
    columns = b[0].shape[1]
    both = mm(a[0], jnp.concatenate(b, axis=1))
    return both[:, :columns] + (both[:, columns:] + mm(a[1], b[0]))


def split3(x):
    high = x.astype(BF16)
    rest = x - high.astype(F32)
    middle = rest.astype(BF16)
    return high, middle, (rest - middle.astype(F32)).astype(BF16)


def mm_exact(exact, b):
    return mm(jnp.concatenate([exact] * len(b), axis=1), jnp.concatenate(b[::-1], axis=0))


def mm6(a, b):
    left = jnp.concatenate([a[0], a[1], a[2], a[0], a[1], a[0]], axis=1)
    right = jnp.concatenate([b[0], b[0], b[0], b[1], b[1], b[2]], axis=0)
    return mm(left, right)


def normed_t(x_t):
    scale = lax.rsqrt(jnp.mean(x_t * x_t, axis=0, keepdims=True) + EPS)
    return x_t * scale, scale


def features_t(seed_t, normed):
    return jnp.exp(mm_exact(seed_t, split3(normed)) * (1.0 / SEED_DIV))


def normed_grad_t(seed, feats_t, dfeats_t, normed, scale):
    grad = mm_exact(seed, split2(dfeats_t * feats_t)) * (1.0 / SEED_DIV)
    return scale * (grad - normed * jnp.mean(grad * normed, axis=0, keepdims=True))


def column_to_rows(column):
    wide = jnp.transpose(jnp.broadcast_to(column, (column.shape[0], 128)))
    row = lax.broadcasted_iota(jnp.int32, (EXT, 128), 0)
    return jnp.where(row == 0, wide[:EXT, :128], wide[:EXT, 128:])


def rows_to_column(block):
    row = jnp.concatenate([block[0:1], block[1:2]], axis=1)
    return jnp.transpose(jnp.broadcast_to(row, (128, row.shape[1])))[:, :1]


def assemble(scratch, refs, member, rows):
    for distance, ref in enumerate(refs):
        place = pl.multiple_of(jnp.bitwise_xor(member, distance) * rows, rows)
        scratch[pl.ds(place, rows), :] = ref[...]


def assemble_sums(scratch, mine_ref, other_ref, index, chips):
    half = mine_ref.shape[0]
    part = half // chips
    for position, ref in ((index[3], mine_ref), (1 - index[3], other_ref)):
        for distance in range(chips):
            place = position * half + jnp.bitwise_xor(index[4], distance) * part
            scratch[pl.ds(pl.multiple_of(place, EXT), part), :] = ref[
                distance * part : (distance + 1) * part
            ]


def split_sums(scratch, mine_out, other_out, index):
    half = mine_out.shape[0]
    mine_out[...] = scratch[pl.ds(pl.multiple_of(index[3] * half, EXT), half), :]
    other_out[...] = scratch[pl.ds(pl.multiple_of((1 - index[3]) * half, EXT), half), :]


def cut_kernel(index, mine_ref, got_ref, *refs):
    parts, total = refs[:-1], refs[-1]
    total[...] = mine_ref[...] + got_ref[...]
    size = parts[0].shape[0]
    for distance, part in enumerate(parts):
        place = jnp.bitwise_xor(index[4], distance) * size
        part[...] = total[pl.ds(pl.multiple_of(place, EXT), size), :]


def gate_row(ext, head, members):
    logits = jnp.concatenate([ext[pl.ds(m * EXT + head, 1), :] for m in range(members)], axis=1)
    return 1.0 / (1.0 + jnp.exp(-logits))


def copy_kernel(moves_of, n_in, *refs):
    index, ins, outs, sems = refs[0], refs[1 : 1 + n_in], refs[1 + n_in : -1], refs[-1]
    copies = [
        pltpu.make_async_copy(source, target, sems.at[position])
        for position, (source, target) in enumerate(moves_of(index, ins, outs))
    ]
    for copy in copies:
        copy.start()
    for copy in copies:
        copy.wait()


def local_copies(moves_of, n_moves, index, ins, out_shapes, name):
    size = sum(math.prod(s.shape) * 4 for s in out_shapes)
    return pl.pallas_call(
        functools.partial(copy_kernel, moves_of, len(ins)),
        grid_spec=pltpu.PrefetchScalarGridSpec(
            num_scalar_prefetch=1,
            grid=(1,),
            in_specs=[pl.BlockSpec(memory_space=pl.ANY)] * len(ins),
            out_specs=[pl.BlockSpec(s.shape, lambda i, ref: (0, 0)) for s in out_shapes],
            scratch_shapes=[pltpu.SemaphoreType.DMA((n_moves,))],
        ),
        out_shape=out_shapes,
        compiler_params=pltpu.CompilerParams(vmem_limit_bytes=32 * 1024 * 1024),
        cost_estimate=pl.CostEstimate(flops=0, bytes_accessed=2 * size, transcendentals=0),
        name=name,
    )(index, *ins)


def sums_kernel(dims, index, *refs):
    members, rows, heads, _, _, _ = dims
    key_refs, value_refs = refs[:members], refs[members : 2 * members]
    seed_t_ref = refs[2 * members]
    keys_out, values_out, mine_out, other_out, low_edge, high_edge, sums_out = refs[
        2 * members + 1 :
    ]
    head = pl.program_id(0)
    member = index[0]
    tokens = members * rows
    reach = rows // 2

    @pl.when(head == 0)
    def _():
        sums_out[pl.ds(heads * 256, sums_out.shape[0] - heads * 256), :] = jnp.zeros(
            (sums_out.shape[0] - heads * 256, 128), F32
        )

    assemble(keys_out, key_refs, member, rows)
    assemble(values_out, value_refs, member, rows)
    keys, values = keys_out[...], values_out[...]
    low_edge[:reach] = keys[:reach]
    low_edge[reach:] = values[:reach]
    high_edge[:reach] = keys[tokens - reach :]
    high_edge[reach:] = values[tokens - reach :]
    normed, _ = normed_t(jnp.transpose(keys))
    feats = features_t(seed_t_ref[...], normed)
    sums_out[pl.ds(pl.multiple_of(head * 256, 256), 256), :] = mm3_wide(split2(feats), split2(values))
    sums_out[pl.ds(pl.multiple_of(heads * 256 + head * EXT, EXT), EXT), :] = column_to_rows(
        jnp.sum(feats, axis=1, keepdims=True)
    )

    @pl.when(head == heads - 1)
    def _():
        split_sums(sums_out, mine_out, other_out, index)


def query_kernel(dims, index, *refs):
    members, rows, heads, chips, _, _ = dims
    query_refs, grad_refs = refs[:members], refs[members : 2 * members]
    ext_refs = refs[2 * members : 3 * members]
    mine_ref, other_ref, seed_ref, seed_t_ref = refs[3 * members : 3 * members + 4]
    low_out, query_out, mine_out, other_out, queries, grads, ext, sums_ref, sums_out = refs[
        3 * members + 4 :
    ]
    head = pl.program_id(0)
    member = index[0]

    @pl.when(head == 0)
    def _():
        assemble(ext, ext_refs, member, EXT)
        assemble_sums(sums_ref, mine_ref, other_ref, index, chips)
        sums_out[pl.ds(heads * 256, sums_out.shape[0] - heads * 256), :] = jnp.zeros(
            (sums_out.shape[0] - heads * 256, 128), F32
        )

    assemble(queries, query_refs, member, rows)
    assemble(grads, grad_refs, member, rows)
    gate = gate_row(ext, head, members)
    sums = sums_ref[pl.ds(pl.multiple_of(head * 256, 256), 256), :]
    totals = rows_to_column(sums_ref[pl.ds(pl.multiple_of(heads * 256 + head * EXT, EXT), EXT), :])
    normed, scale = normed_t(jnp.transpose(queries[...]))
    feats = features_t(seed_t_ref[...], normed)
    feats_parts = split2(feats)
    inverse = 1.0 / jnp.sum(feats * totals, axis=0, keepdims=True)
    low = mm3_tall(split2(jnp.transpose(sums)), feats_parts) * inverse
    dnum = jnp.transpose(grads[...]) * ((1.0 - gate) * inverse)
    dden = -jnp.sum(dnum * low, axis=0, keepdims=True)
    dfeats = mm3_deep(split2(sums), split2(dnum)) + totals * dden
    low_out[...] = low
    query_out[...] = normed_grad_t(seed_ref[...], feats, dfeats, normed, scale)
    sums_out[pl.ds(pl.multiple_of(head * 256, 256), 256), :] = mm3_wide(
        feats_parts, split2(jnp.transpose(dnum))
    )
    sums_out[pl.ds(pl.multiple_of(heads * 256 + head * EXT, EXT), EXT), :] = column_to_rows(
        jnp.sum(feats * dden, axis=1, keepdims=True)
    )

    @pl.when(head == heads - 1)
    def _():
        split_sums(sums_out, mine_out, other_out, index)


def fill_bias(bias, ext, members, rows, first, last):
    reach = rows // 2
    key_at = lax.broadcasted_iota(jnp.int32, (rows, rows), 0)
    query_at = lax.broadcasted_iota(jnp.int32, (rows, rows), 1)
    for block in range(members):
        for other in range(members):
            gap = (other - block) * rows + key_at - query_at
            allowed = jnp.abs(gap) <= reach
            if other != block:
                flag = ext[block * EXT + EXT - 1 : block * EXT + EXT, other : other + 1]
                allowed = jnp.logical_or(allowed, jnp.broadcast_to(flag, (rows, rows)) > 0.5)
            bias[other * rows : (other + 1) * rows, block * rows : (block + 1) * rows] = jnp.where(
                allowed, 0.0, NEG_FILL
            )
        allowed = jnp.zeros((rows, rows), jnp.bool_)
        if block == 0:
            allowed = (key_at < reach) & (query_at <= key_at) & (first == 0)
        if block == members - 1:
            right = (key_at >= reach) & (query_at >= key_at) & (last == 0)
            allowed = jnp.logical_or(allowed, right)
        bias[members * rows :, block * rows : (block + 1) * rows] = jnp.where(
            allowed, 0.0, NEG_FILL
        )


def sparse_kernel(dims, index, *refs):
    members, rows, heads, _, start, _ = dims
    query_refs, grad_refs = refs[:members], refs[members : 2 * members]
    ext_refs = refs[2 * members : 3 * members]
    keys_ref, values_ref, left_ref, right_ref, low_ref, query_low_ref = refs[
        3 * members : 3 * members + 6
    ]
    outs = refs[3 * members + 6 :]
    messages = outs[:members]
    keys_out, values_out, left_out, right_out = outs[members : members + 4]
    queries, grads, ext, bias, keys_all, values_all = outs[members + 4 :]
    step = pl.program_id(0)
    head = step + start
    member = index[0]
    tokens = members * rows
    reach = rows // 2

    @pl.when(step == 0)
    def _():
        assemble(ext, ext_refs, member, EXT)
        fill_bias(bias, ext, members, rows, index[1], index[2])
        for message in messages:
            message[pl.ds(2 * heads * rows, EXT), :] = jnp.zeros((EXT, 128), F32)

    assemble(queries, query_refs, member, rows)
    assemble(grads, grad_refs, member, rows)
    keys_all[:tokens] = keys_ref[...]
    keys_all[tokens : tokens + reach] = left_ref[:reach]
    keys_all[tokens + reach :] = right_ref[:reach]
    values_all[:tokens] = values_ref[...]
    values_all[tokens : tokens + reach] = left_ref[reach:]
    values_all[tokens + reach :] = right_ref[reach:]

    gate = gate_row(ext, head, members)
    root = 1.0 / math.sqrt(HEAD_DIM)
    values = split2(values_all[...])
    keys_t = split2(jnp.transpose(keys_all[...]))
    values_t = split2(jnp.transpose(values_all[...]))
    scaled = queries[...] * root
    scores = mm6(split3(keys_all[...]), split3(jnp.transpose(scaled))) + bias[...]
    weights = jnp.exp(scores - jnp.max(scores, axis=0, keepdims=True))
    inverse = 1.0 / jnp.sum(weights, axis=0, keepdims=True)
    weight_parts = split2(weights)
    mixed = mm3_tall(values_t, weight_parts) * inverse
    low = low_ref[...]
    grad_t = jnp.transpose(grads[...])
    gate_grad = jnp.sum(grad_t * (mixed - low), axis=0, keepdims=True) * gate * (1.0 - gate)
    sparse_grad = grad_t * (gate * inverse)
    delta = jnp.sum(sparse_grad * mixed, axis=0, keepdims=True)
    score_grad = weights * (mm3_deep(values, split2(sparse_grad)) - delta)
    score_parts = split2(score_grad)
    query_grad = mm3_tall(keys_t, score_parts) * root + query_low_ref[...]
    keys_grad = mm3_wide(score_parts, split2(scaled))
    values_grad = mm3_wide(weight_parts, split2(jnp.transpose(sparse_grad)))
    keys_out[...] = keys_grad[:tokens]
    values_out[...] = values_grad[:tokens]
    left_out[:reach] = keys_grad[tokens : tokens + reach]
    left_out[reach:] = values_grad[tokens : tokens + reach]
    right_out[:reach] = keys_grad[tokens + reach :]
    right_out[reach:] = values_grad[tokens + reach :]
    queries[...] = jnp.transpose(gate * mixed + (1.0 - gate) * low)
    grads[...] = jnp.transpose(query_grad)
    for m in range(members):
        ext[pl.ds(m * EXT + head, 1), :] = gate_grad[:, m * rows : (m + 1) * rows]
    for distance, message in enumerate(messages):
        other = jnp.bitwise_xor(member, distance)
        place = pl.ds(pl.multiple_of(other * rows, rows), rows)
        at = pl.multiple_of(step * 2 * rows, rows)
        message[pl.ds(at, rows), :] = queries[place, :]
        message[pl.ds(at + rows, rows), :] = grads[place, :]

    @pl.when(step == heads - 1)
    def _():
        for distance, message in enumerate(messages):
            other = jnp.bitwise_xor(member, distance)
            message[pl.ds(2 * heads * rows, EXT), :] = ext[
                pl.ds(pl.multiple_of(other * EXT, EXT), EXT), :
            ]


def keys_kernel(dims, index, *refs):
    members, rows, _, chips, start, heads = dims
    keys_ref, values_ref, mine_ref, other_ref, keys_grad, values_grad = refs[:6]
    left_ref, right_ref, seed_ref, seed_t_ref = refs[6:10]
    messages = refs[10 : 10 + members]
    dkeys, dvalues, sums_ref = refs[10 + members :]
    step = pl.program_id(0)
    head = step + start
    member = index[0]
    tokens = members * rows
    reach = rows // 2

    @pl.when(step == 0)
    def _():
        assemble_sums(sums_ref, mine_ref, other_ref, index, chips)

    sums = sums_ref[pl.ds(pl.multiple_of(head * 256, 256), 256), :]
    totals = rows_to_column(sums_ref[pl.ds(pl.multiple_of(heads * 256 + head * EXT, EXT), EXT), :])
    normed, scale = normed_t(jnp.transpose(keys_ref[...]))
    feats = features_t(seed_t_ref[...], normed)
    dfeats = mm3_deep(split2(sums), split2(jnp.transpose(values_ref[...]))) + totals
    key_low = normed_grad_t(seed_ref[...], feats, dfeats, normed, scale)
    value_low = mm3_tall(split2(jnp.transpose(sums)), split2(feats))
    dkeys[...] = keys_grad[...] + jnp.transpose(key_low)
    dvalues[...] = values_grad[...] + jnp.transpose(value_low)
    dkeys[:reach] += left_ref[:reach]
    dvalues[:reach] += left_ref[reach:]
    dkeys[tokens - reach :] += right_ref[:reach]
    dvalues[tokens - reach :] += right_ref[reach:]
    for distance, message in enumerate(messages):
        other = jnp.bitwise_xor(member, distance)
        place = pl.ds(pl.multiple_of(other * rows, rows), rows)
        message[:rows] = dkeys[place, :]
        message[rows:] = dvalues[place, :]


def per_head_call(kernel, dims, index, ins, outs, scratch, flops, exps, name):
    heads = dims[2]
    size = sum(math.prod(s.shape) * 4 for s, _ in outs)
    return pl.pallas_call(
        functools.partial(kernel, dims),
        grid_spec=pltpu.PrefetchScalarGridSpec(
            num_scalar_prefetch=1,
            grid=(heads,),
            in_specs=[spec for _, spec in ins],
            out_specs=[spec for _, spec in outs],
            scratch_shapes=scratch,
        ),
        out_shape=[shape for shape, _ in outs],
        compiler_params=pltpu.CompilerParams(
            vmem_limit_bytes=56 * 1024 * 1024, dimension_semantics=("arbitrary",)
        ),
        cost_estimate=pl.CostEstimate(
            flops=flops * heads, bytes_accessed=2 * size, transcendentals=exps * heads
        ),
        name=name,
    )(index, *[x for x, _ in ins])


def swap(block, axis, distance):
    return lax.ppermute(block, axis, [(i, i ^ distance) for i in range(lax.axis_size(axis))])


def cut_sums(index, mine, got):
    chips = lax.axis_size("seq") // 2
    part = jax.ShapeDtypeStruct((mine.shape[0] // chips, 128), F32)
    return pl.pallas_call(
        cut_kernel,
        grid_spec=pltpu.PrefetchScalarGridSpec(
            num_scalar_prefetch=1,
            grid=(1,),
            in_specs=[pl.BlockSpec(mine.shape, lambda i, ref: (0, 0))] * 2,
            out_specs=[pl.BlockSpec(part.shape, lambda i, ref: (0, 0))] * chips,
            scratch_shapes=[pltpu.VMEM(mine.shape, F32)],
        ),
        out_shape=[part] * chips,
        cost_estimate=pl.CostEstimate(
            flops=mine.size, bytes_accessed=12 * mine.size, transcendentals=0
        ),
        name="cut_sums",
    )(index, mine, got)


def reduce_parts(parts):
    own = parts[0]
    for d, part in enumerate(parts[1:], 1):
        own = own + swap(part, "seq", 2 * d)
    return own


def gather_parts(own):
    chips = lax.axis_size("seq") // 2
    return jnp.concatenate([own] + [swap(own, "seq", 2 * d) for d in range(1, chips)], axis=0)


def after(value, *others):
    return lax.optimization_barrier((value, *others))[0]


def to_next(block):
    count = lax.axis_size("seq")
    return lax.ppermute(block, "seq", [(i, i + 1) for i in range(count - 1)])


def to_previous(block):
    count = lax.axis_size("seq")
    return lax.ppermute(block, "seq", [(i + 1, i) for i in range(count - 1)])


def shards(
    queries,
    key_matrix,
    value_matrix,
    gate_logits,
    output_grad,
    cycle_offsets,
    block_count,
    feature_seed,
):
    rows, width = queries.shape
    members = lax.axis_size("blk")
    member = lax.axis_index("blk")
    groups = lax.axis_size("seq")
    group = lax.axis_index("seq")
    chips = groups // 2
    heads = gate_logits.shape[1] // members
    tokens = members * rows
    others = range(1, members)
    index = jnp.stack(
        [
            member,
            (group == 0).astype(jnp.int32),
            (group == groups - 1).astype(jnp.int32),
            group & 1,
            group >> 1,
        ]
    ).astype(jnp.int32)
    sum_rows = -(-(heads * (256 + EXT)) // (EXT * groups)) * EXT * groups
    chunks = [(0, heads // 2), (heads // 2, heads - heads // 2)]
    dims = (members, rows, heads, chips, 0, heads)

    def shape(*sizes):
        return jax.ShapeDtypeStruct(sizes, F32)

    def block_of(message_rows, at):
        return pl.BlockSpec((message_rows, 128), lambda h, ref: (at(h, ref), 0))

    def per_head(block, start=0):
        return pl.BlockSpec(block, lambda h, ref: (h + start, 0))

    def whole(x):
        return pl.BlockSpec(x.shape, lambda h, ref: (0,) * len(x.shape))

    def packing(index, ins, outs, extra):
        moves = []
        for d, out in zip(others, outs):
            other = jnp.bitwise_xor(index[0], d)
            for a in range(2):
                for h in range(heads):
                    column = pl.multiple_of((other * heads + h) * 128, 128)
                    moves.append(
                        (
                            ins[a].at[:, pl.ds(column, 128)],
                            out.at[pl.ds((a * heads + h) * rows, rows), :],
                        )
                    )
            if extra:
                start = pl.multiple_of(other * EXT, EXT)
                moves.append(
                    (ins[2].at[pl.ds(start, EXT), :], out.at[pl.ds(2 * heads * rows, EXT), :])
                )
        return moves

    def unpacking(index, ins, outs):
        moves = []
        for chunk, (start, count) in enumerate(chunks):
            for d in range(members):
                other = jnp.bitwise_xor(index[0], d)
                message = ins[chunk * members + d]
                for a in range(2):
                    for h in range(count):
                        column = pl.multiple_of((other * heads + start + h) * 128, 128)
                        moves.append(
                            (
                                message.at[pl.ds((2 * h + a) * rows, rows), :],
                                outs[a].at[:, pl.ds(column, 128)],
                            )
                        )
        return moves

    kv_sent = local_copies(
        functools.partial(packing, extra=False),
        2 * heads * (members - 1),
        index,
        [key_matrix, value_matrix],
        [shape(2 * heads * rows, 128)] * (members - 1),
        "pack_kv",
    )
    kv = [swap(block, "blk", d) for d, block in zip(others, kv_sent)]

    active = jnp.arange(cycle_offsets.shape[1], dtype=jnp.int32) < block_count[0]
    named = jnp.mod(cycle_offsets[0] + member, members)
    lanes = jnp.arange(128, dtype=jnp.int32)
    flags = jnp.any(active[:, None] & (named[:, None] == lanes[None, :]), axis=0).astype(F32)
    logits = jnp.transpose(gate_logits).reshape(members, heads, rows)
    ext = jnp.concatenate(
        [
            logits,
            jnp.zeros((members, EXT - 1 - heads, rows), F32),
            jnp.broadcast_to(flags[None, None, :], (members, 1, 128)),
        ],
        axis=1,
    ).reshape(members * EXT, 128)
    qd_sent = local_copies(
        functools.partial(packing, extra=True),
        (2 * heads + 1) * (members - 1),
        index,
        [queries, output_grad, ext],
        [shape(2 * heads * rows + EXT, 128)] * (members - 1),
        "pack_qd",
    )
    kv, qd_sent = lax.optimization_barrier((kv, qd_sent))
    qd = [swap(block, "blk", d) for d, block in zip(others, qd_sent)]

    seed = feature_seed.astype(BF16)
    seed_t = jnp.transpose(feature_seed).astype(BF16)
    unit = 2 * tokens * 128 * 256
    exps = tokens * 256
    half = shape(sum_rows // 2, 128)
    all_sums = pltpu.VMEM((sum_rows, 128), F32)
    own_spec = pl.BlockSpec((rows, 128), lambda h, ref: (0, ref[0] * heads + h))
    keys_full, values_full, sums, sums_other, low_edge, high_edge = per_head_call(
        sums_kernel,
        dims,
        index,
        [(key_matrix, own_spec)]
        + [(x, per_head((rows, 128))) for x in kv]
        + [(value_matrix, own_spec)]
        + [(x, per_head((rows, 128), heads)) for x in kv]
        + [(seed_t, whole(seed_t))],
        [
            (shape(heads * tokens, 128), per_head((tokens, 128))),
            (shape(heads * tokens, 128), per_head((tokens, 128))),
            (half, whole(half)),
            (half, whole(half)),
            (shape(heads * rows, 128), per_head((rows, 128))),
            (shape(heads * rows, 128), per_head((rows, 128))),
        ],
        [all_sums],
        6 * unit,
        exps,
        "key_sums",
    )
    right_halo = to_previous(low_edge)
    left_halo = to_next(high_edge)
    sums = reduce_parts(cut_sums(index, sums, swap(sums_other, "seq", 1)))
    sums, *qd[:2] = lax.optimization_barrier((sums, *qd[:2]))
    sums = gather_parts(sums)
    sums_other = swap(sums, "seq", 1)

    ext_block = block_of(EXT, lambda h, ref: 2 * heads * rows // EXT)

    def query_side(start):
        own = pl.BlockSpec((rows, 128), lambda h, ref: (0, ref[0] * heads + start + h))
        return (
            [(queries, own)]
            + [(x, per_head((rows, 128), start)) for x in qd]
            + [(output_grad, own)]
            + [(x, per_head((rows, 128), heads + start)) for x in qd]
            + [(ext, block_of(EXT, lambda h, ref: ref[0]))]
            + [(x, ext_block) for x in qd]
        )

    row_scratch = [
        pltpu.VMEM((tokens, 128), F32),
        pltpu.VMEM((tokens, 128), F32),
        pltpu.VMEM((members * EXT, 128), F32),
    ]
    low, query_low, sums_grad, grad_other = per_head_call(
        query_kernel,
        dims,
        index,
        query_side(0)
        + [
            (sums, whole(sums)),
            (sums_other, whole(sums_other)),
            (seed, whole(seed)),
            (seed_t, whole(seed_t)),
        ],
        [
            (shape(heads * 128, tokens), per_head((128, tokens))),
            (shape(heads * 128, tokens), per_head((128, tokens))),
            (half, whole(half)),
            (half, whole(half)),
        ],
        row_scratch + [all_sums, all_sums],
        14 * unit,
        exps,
        "query_low_rank",
    )

    def sparse(chunk, low, query_low):
        start, count = chunks[chunk]
        message = shape(2 * count * rows + EXT, 128)
        outs = per_head_call(
            sparse_kernel,
            (members, rows, count, chips, start, heads),
            index,
            query_side(start)
            + [
                (keys_full, per_head((tokens, 128), start)),
                (values_full, per_head((tokens, 128), start)),
                (left_halo, per_head((rows, 128), start)),
                (right_halo, per_head((rows, 128), start)),
                (low, per_head((128, tokens), start)),
                (query_low, per_head((128, tokens), start)),
            ],
            [(message, whole(message))] * members
            + [(shape(count * tokens, 128), per_head((tokens, 128)))] * 2
            + [(shape(count * rows, 128), per_head((rows, 128)))] * 2,
            row_scratch
            + [
                pltpu.VMEM((tokens + rows, tokens), F32),
                pltpu.VMEM((tokens + rows, 128), F32),
                pltpu.VMEM((tokens + rows, 128), F32),
            ],
            42 * tokens * (tokens + rows) * 128,
            tokens * (tokens + rows),
            "sparse",
        )
        return outs[:members], outs[members:]

    def key_side(chunk, parts, sums, sums_other):
        start, count = chunks[chunk]
        keys_sparse, values_sparse, left_grad, right_grad = parts
        back_right = to_previous(left_grad)
        back_left = to_next(right_grad)
        message = shape(2 * count * rows, 128)
        return per_head_call(
            keys_kernel,
            (members, rows, count, chips, start, heads),
            index,
            [
                (keys_full, per_head((tokens, 128), start)),
                (values_full, per_head((tokens, 128), start)),
                (sums, whole(sums)),
                (sums_other, whole(sums_other)),
                (keys_sparse, per_head((tokens, 128))),
                (values_sparse, per_head((tokens, 128))),
                (back_left, per_head((rows, 128))),
                (back_right, per_head((rows, 128))),
                (seed, whole(seed)),
                (seed_t, whole(seed_t)),
            ],
            [(message, per_head((2 * rows, 128)))] * members,
            [pltpu.VMEM((tokens, 128), F32), pltpu.VMEM((tokens, 128), F32), all_sums],
            13 * unit,
            exps,
            "key_low_rank",
        )

    def back(messages):
        return [messages[0]] + [swap(block, "blk", d) for d, block in zip(others, messages[1:])]

    parts = cut_sums(index, sums_grad, swap(grad_other, "seq", 1))
    low, query_low, *parts = lax.optimization_barrier((low, query_low, *parts))
    od_first, keys_first = sparse(0, low, query_low)
    own = reduce_parts(parts)
    low, query_low, own, *od_first = lax.optimization_barrier((low, query_low, own, *od_first))
    od_first = back(od_first)
    od_second, keys_second = sparse(1, low, query_low)
    sums = gather_parts(own)
    sums, *od_second = lax.optimization_barrier((sums, *od_second))
    sums_other = swap(sums, "seq", 1)
    od_second = back(od_second)
    dkv_first = back(key_side(0, keys_first, sums, sums_other))
    dkv_second = back(key_side(1, keys_second, sums, sums_other))

    od = od_first + od_second
    n_moves = 2 * heads * members
    attended, query_grad = local_copies(
        unpacking, n_moves, index, od, [shape(rows, width)] * 2, "unpack_od"
    )
    gate_parts = []
    for chunk, (start, count) in enumerate(chunks):
        rows_back = jnp.zeros((members, EXT, 128), F32)
        for d in range(members):
            block = od[chunk * members + d]
            rows_back = lax.dynamic_update_slice_in_dim(
                rows_back, block[None, 2 * count * rows :, :], member ^ d, 0
            )
        gate_parts.append(rows_back[:, start : start + count, :])
    gate_grad = jnp.concatenate(gate_parts, axis=1).reshape(members * heads, rows)
    key_grad, value_grad = local_copies(
        unpacking,
        n_moves,
        index,
        dkv_first + dkv_second,
        [shape(rows, width)] * 2,
        "unpack_kv",
    )
    return (attended, query_grad, key_grad, value_grad, jnp.transpose(gate_grad))


def solution(mesh):
    row_spec = P(("seq", "blk"), None)
    return jax.shard_map(
        shards,
        mesh=mesh,
        in_specs=(row_spec,) * 6 + (P(("seq", "blk")), P()),
        out_specs=(row_spec,) * 5,
        check_vma=False,
    )
```

```python
import functools
import math

import jax
import jax.numpy as jnp
from jax import lax
from jax.experimental import pallas as pl
from jax.experimental.pallas import tpu as pltpu
from jax.sharding import PartitionSpec as P

HEAD_DIM = 128
EXT = 8
NEG_FILL = -1e30
SEED_DIV = 13.0
EPS = 1e-06
F32 = jnp.float32
BF16 = jnp.bfloat16


def split2(x):
    high = x.astype(BF16)
    return high, (x - high.astype(F32)).astype(BF16)


def mm(a, b):
    return lax.dot_general(a, b, (((1,), (0,)), ((), ())), preferred_element_type=F32)


def mm3_deep(a, b):
    return mm(
        jnp.concatenate([a[0], a[1], a[0]], axis=1), jnp.concatenate([b[0], b[0], b[1]], axis=0)
    )


def mm3_tall(a, b):
    rows = a[0].shape[0]
    both = mm(jnp.concatenate(a, axis=0), b[0])
    return both[:rows] + (both[rows:] + mm(a[0], b[1]))


def mm3_wide(a, b):
    columns = b[0].shape[1]
    both = mm(a[0], jnp.concatenate(b, axis=1))
    return both[:, :columns] + (both[:, columns:] + mm(a[1], b[0]))


def split3(x):
    high = x.astype(BF16)
    rest = x - high.astype(F32)
    middle = rest.astype(BF16)
    return high, middle, (rest - middle.astype(F32)).astype(BF16)


def mm_exact(exact, b):
    return mm(jnp.concatenate([exact] * len(b), axis=1), jnp.concatenate(b[::-1], axis=0))


def mm6(a, b):
    left = jnp.concatenate([a[0], a[1], a[2], a[0], a[1], a[0]], axis=1)
    right = jnp.concatenate([b[0], b[0], b[0], b[1], b[1], b[2]], axis=0)
    return mm(left, right)


def normed_t(x_t):
    scale = lax.rsqrt(jnp.mean(x_t * x_t, axis=0, keepdims=True) + EPS)
    return x_t * scale, scale


def features_t(seed_t, normed):
    return jnp.exp(mm_exact(seed_t, split3(normed)) * (1.0 / SEED_DIV))


def normed_grad_t(seed, feats_t, dfeats_t, normed, scale):
    grad = mm_exact(seed, split2(dfeats_t * feats_t)) * (1.0 / SEED_DIV)
    return scale * (grad - normed * jnp.mean(grad * normed, axis=0, keepdims=True))


def column_to_rows(column):
    wide = jnp.transpose(jnp.broadcast_to(column, (column.shape[0], 128)))
    row = lax.broadcasted_iota(jnp.int32, (EXT, 128), 0)
    return jnp.where(row == 0, wide[:EXT, :128], wide[:EXT, 128:])


def rows_to_column(block):
    row = jnp.concatenate([block[0:1], block[1:2]], axis=1)
    return jnp.transpose(jnp.broadcast_to(row, (128, row.shape[1])))[:, :1]


def assemble(scratch, refs, member, rows):
    for distance, ref in enumerate(refs):
        place = pl.multiple_of(jnp.bitwise_xor(member, distance) * rows, rows)
        scratch[pl.ds(place, rows), :] = ref[...]


def assemble_sums(scratch, mine_ref, other_ref, index, chips):
    half = mine_ref.shape[0]
    part = half // chips
    for position, ref in ((index[3], mine_ref), (1 - index[3], other_ref)):
        for distance in range(chips):
            place = position * half + jnp.bitwise_xor(index[4], distance) * part
            scratch[pl.ds(pl.multiple_of(place, EXT), part), :] = ref[
                distance * part : (distance + 1) * part
            ]


def split_sums(scratch, mine_out, other_out, index):
    half = mine_out.shape[0]
    mine_out[...] = scratch[pl.ds(pl.multiple_of(index[3] * half, EXT), half), :]
    other_out[...] = scratch[pl.ds(pl.multiple_of((1 - index[3]) * half, EXT), half), :]


def cut_kernel(index, mine_ref, got_ref, *refs):
    parts, total = refs[:-1], refs[-1]
    total[...] = mine_ref[...] + got_ref[...]
    size = parts[0].shape[0]
    for distance, part in enumerate(parts):
        place = jnp.bitwise_xor(index[4], distance) * size
        part[...] = total[pl.ds(pl.multiple_of(place, EXT), size), :]


def gate_row(ext, head, members):
    logits = jnp.concatenate([ext[pl.ds(m * EXT + head, 1), :] for m in range(members)], axis=1)
    return 1.0 / (1.0 + jnp.exp(-logits))


def copy_kernel(moves_of, n_in, *refs):
    index, ins, outs, sems = refs[0], refs[1 : 1 + n_in], refs[1 + n_in : -1], refs[-1]
    copies = [
        pltpu.make_async_copy(source, target, sems.at[position])
        for position, (source, target) in enumerate(moves_of(index, ins, outs))
    ]
    for copy in copies:
        copy.start()
    for copy in copies:
        copy.wait()


def local_copies(moves_of, n_moves, index, ins, out_shapes, name):
    size = sum(math.prod(s.shape) * 4 for s in out_shapes)
    return pl.pallas_call(
        functools.partial(copy_kernel, moves_of, len(ins)),
        grid_spec=pltpu.PrefetchScalarGridSpec(
            num_scalar_prefetch=1,
            grid=(1,),
            in_specs=[pl.BlockSpec(memory_space=pl.ANY)] * len(ins),
            out_specs=[pl.BlockSpec(s.shape, lambda i, ref: (0, 0)) for s in out_shapes],
            scratch_shapes=[pltpu.SemaphoreType.DMA((n_moves,))],
        ),
        out_shape=out_shapes,
        compiler_params=pltpu.CompilerParams(vmem_limit_bytes=32 * 1024 * 1024),
        cost_estimate=pl.CostEstimate(flops=0, bytes_accessed=2 * size, transcendentals=0),
        name=name,
    )(index, *ins)


def tile_kernel(moves_of, n_in, n_out, index, *refs):
    ins, outs = refs[:n_in], refs[-3 - n_out : -3]
    tiles, in_sems, out_sems = refs[-3:]
    moves = moves_of(index, ins, outs)
    loads, stores = [], []
    for position, (source, target) in enumerate(moves):
        tile = tiles.at[position, pl.ds(0, source.shape[0]), :]
        loads.append(pltpu.make_async_copy(source, tile, in_sems.at[position]))
        stores.append(pltpu.make_async_copy(tile, target, out_sems.at[position]))
    for load in loads:
        load.start()
    for load, store in zip(loads, stores):
        load.wait()
        store.start()
    for store in stores:
        store.wait()


def tile_copies(moves_of, n_moves, index, ins, out_shapes, name):
    size = n_moves * 128 * 128 * 4
    return pl.pallas_call(
        functools.partial(tile_kernel, moves_of, len(ins), len(out_shapes)),
        grid_spec=pltpu.PrefetchScalarGridSpec(
            num_scalar_prefetch=1,
            grid=(1,),
            in_specs=[pl.BlockSpec(memory_space=pl.ANY)] * len(ins),
            out_specs=[pl.BlockSpec(memory_space=pl.ANY)] * len(out_shapes),
            scratch_shapes=[
                pltpu.VMEM((n_moves, 128, 128), F32),
                pltpu.SemaphoreType.DMA((n_moves,)),
                pltpu.SemaphoreType.DMA((n_moves,)),
            ],
        ),
        out_shape=out_shapes,
        compiler_params=pltpu.CompilerParams(vmem_limit_bytes=56 * 1024 * 1024),
        cost_estimate=pl.CostEstimate(flops=0, bytes_accessed=2 * size, transcendentals=0),
        name=name,
    )(index, *ins)


def sums_kernel(dims, index, *refs):
    members, rows, heads, _, _, _ = dims
    key_refs, value_refs = refs[:members], refs[members : 2 * members]
    seed_t_ref = refs[2 * members]
    keys_out, values_out, mine_out, other_out, low_edge, high_edge, sums_out = refs[
        2 * members + 1 :
    ]
    head = pl.program_id(0)
    member = index[0]
    tokens = members * rows
    reach = rows // 2

    @pl.when(head == 0)
    def _():
        sums_out[pl.ds(heads * 256, sums_out.shape[0] - heads * 256), :] = jnp.zeros(
            (sums_out.shape[0] - heads * 256, 128), F32
        )

    assemble(keys_out, key_refs, member, rows)
    assemble(values_out, value_refs, member, rows)
    keys, values = keys_out[...], values_out[...]
    low_edge[:reach] = keys[:reach]
    low_edge[reach:] = values[:reach]
    high_edge[:reach] = keys[tokens - reach :]
    high_edge[reach:] = values[tokens - reach :]
    normed, _ = normed_t(jnp.transpose(keys))
    feats = features_t(seed_t_ref[...], normed)
    sums_out[pl.ds(pl.multiple_of(head * 256, 256), 256), :] = mm3_wide(split2(feats), split2(values))
    sums_out[pl.ds(pl.multiple_of(heads * 256 + head * EXT, EXT), EXT), :] = column_to_rows(
        jnp.sum(feats, axis=1, keepdims=True)
    )

    @pl.when(head == heads - 1)
    def _():
        split_sums(sums_out, mine_out, other_out, index)


def query_kernel(dims, index, *refs):
    members, rows, heads, chips, _, _ = dims
    query_refs, grad_refs = refs[:members], refs[members : 2 * members]
    ext_refs = refs[2 * members : 3 * members]
    mine_ref, other_ref, seed_ref, seed_t_ref = refs[3 * members : 3 * members + 4]
    low_out, query_out, mine_out, other_out, queries, grads, ext, sums_ref, sums_out = refs[
        3 * members + 4 :
    ]
    head = pl.program_id(0)
    member = index[0]

    @pl.when(head == 0)
    def _():
        assemble(ext, ext_refs, member, EXT)
        assemble_sums(sums_ref, mine_ref, other_ref, index, chips)
        sums_out[pl.ds(heads * 256, sums_out.shape[0] - heads * 256), :] = jnp.zeros(
            (sums_out.shape[0] - heads * 256, 128), F32
        )

    assemble(queries, query_refs, member, rows)
    assemble(grads, grad_refs, member, rows)
    gate = gate_row(ext, head, members)
    sums = sums_ref[pl.ds(pl.multiple_of(head * 256, 256), 256), :]
    totals = rows_to_column(sums_ref[pl.ds(pl.multiple_of(heads * 256 + head * EXT, EXT), EXT), :])
    normed, scale = normed_t(jnp.transpose(queries[...]))
    feats = features_t(seed_t_ref[...], normed)
    feats_parts = split2(feats)
    inverse = 1.0 / jnp.sum(feats * totals, axis=0, keepdims=True)
    low = mm3_tall(split2(jnp.transpose(sums)), feats_parts) * inverse
    dnum = jnp.transpose(grads[...]) * ((1.0 - gate) * inverse)
    dden = -jnp.sum(dnum * low, axis=0, keepdims=True)
    dfeats = mm3_deep(split2(sums), split2(dnum)) + totals * dden
    low_out[...] = low
    query_out[...] = normed_grad_t(seed_ref[...], feats, dfeats, normed, scale)
    sums_out[pl.ds(pl.multiple_of(head * 256, 256), 256), :] = mm3_wide(
        feats_parts, split2(jnp.transpose(dnum))
    )
    sums_out[pl.ds(pl.multiple_of(heads * 256 + head * EXT, EXT), EXT), :] = column_to_rows(
        jnp.sum(feats * dden, axis=1, keepdims=True)
    )

    @pl.when(head == heads - 1)
    def _():
        split_sums(sums_out, mine_out, other_out, index)


def fill_bias(bias, ext, members, rows, first, last):
    reach = rows // 2
    key_at = lax.broadcasted_iota(jnp.int32, (rows, rows), 0)
    query_at = lax.broadcasted_iota(jnp.int32, (rows, rows), 1)
    for block in range(members):
        for other in range(members):
            gap = (other - block) * rows + key_at - query_at
            allowed = jnp.abs(gap) <= reach
            if other != block:
                flag = ext[block * EXT + EXT - 1 : block * EXT + EXT, other : other + 1]
                allowed = jnp.logical_or(allowed, jnp.broadcast_to(flag, (rows, rows)) > 0.5)
            bias[other * rows : (other + 1) * rows, block * rows : (block + 1) * rows] = jnp.where(
                allowed, 0.0, NEG_FILL
            )
        allowed = jnp.zeros((rows, rows), jnp.bool_)
        if block == 0:
            allowed = (key_at < reach) & (query_at <= key_at) & (first == 0)
        if block == members - 1:
            right = (key_at >= reach) & (query_at >= key_at) & (last == 0)
            allowed = jnp.logical_or(allowed, right)
        bias[members * rows :, block * rows : (block + 1) * rows] = jnp.where(
            allowed, 0.0, NEG_FILL
        )


def sparse_kernel(dims, index, *refs):
    members, rows, heads, _, start, _ = dims
    query_refs, grad_refs = refs[:members], refs[members : 2 * members]
    ext_refs = refs[2 * members : 3 * members]
    keys_ref, values_ref, left_ref, right_ref, low_ref, query_low_ref = refs[
        3 * members : 3 * members + 6
    ]
    outs = refs[3 * members + 6 :]
    messages = outs[:members]
    keys_out, values_out, left_out, right_out = outs[members : members + 4]
    queries, grads, ext, bias, keys_all, values_all = outs[members + 4 :]
    step = pl.program_id(0)
    head = step + start
    member = index[0]
    tokens = members * rows
    reach = rows // 2

    @pl.when(step == 0)
    def _():
        assemble(ext, ext_refs, member, EXT)
        fill_bias(bias, ext, members, rows, index[1], index[2])
        for message in messages:
            message[pl.ds(2 * heads * rows, EXT), :] = jnp.zeros((EXT, 128), F32)

    assemble(queries, query_refs, member, rows)
    assemble(grads, grad_refs, member, rows)
    keys_all[:tokens] = keys_ref[...]
    keys_all[tokens : tokens + reach] = left_ref[:reach]
    keys_all[tokens + reach :] = right_ref[:reach]
    values_all[:tokens] = values_ref[...]
    values_all[tokens : tokens + reach] = left_ref[reach:]
    values_all[tokens + reach :] = right_ref[reach:]

    gate = gate_row(ext, head, members)
    root = 1.0 / math.sqrt(HEAD_DIM)
    values = split2(values_all[...])
    keys_t = split2(jnp.transpose(keys_all[...]))
    values_t = split2(jnp.transpose(values_all[...]))
    scaled = queries[...] * root
    scores = mm6(split3(keys_all[...]), split3(jnp.transpose(scaled))) + bias[...]
    weights = jnp.exp(scores - jnp.max(scores, axis=0, keepdims=True))
    inverse = 1.0 / jnp.sum(weights, axis=0, keepdims=True)
    weight_parts = split2(weights)
    mixed = mm3_tall(values_t, weight_parts) * inverse
    low = low_ref[...]
    grad_t = jnp.transpose(grads[...])
    gate_grad = jnp.sum(grad_t * (mixed - low), axis=0, keepdims=True) * gate * (1.0 - gate)
    sparse_grad = grad_t * (gate * inverse)
    delta = jnp.sum(sparse_grad * mixed, axis=0, keepdims=True)
    score_grad = weights * (mm3_deep(values, split2(sparse_grad)) - delta)
    score_parts = split2(score_grad)
    query_grad = mm3_tall(keys_t, score_parts) * root + query_low_ref[...]
    keys_grad = mm3_wide(score_parts, split2(scaled))
    values_grad = mm3_wide(weight_parts, split2(jnp.transpose(sparse_grad)))
    keys_out[...] = keys_grad[:tokens]
    values_out[...] = values_grad[:tokens]
    left_out[:reach] = keys_grad[tokens : tokens + reach]
    left_out[reach:] = values_grad[tokens : tokens + reach]
    right_out[:reach] = keys_grad[tokens + reach :]
    right_out[reach:] = values_grad[tokens + reach :]
    queries[...] = jnp.transpose(gate * mixed + (1.0 - gate) * low)
    grads[...] = jnp.transpose(query_grad)
    for m in range(members):
        ext[pl.ds(m * EXT + head, 1), :] = gate_grad[:, m * rows : (m + 1) * rows]
    for distance, message in enumerate(messages):
        other = jnp.bitwise_xor(member, distance)
        place = pl.ds(pl.multiple_of(other * rows, rows), rows)
        at = pl.multiple_of(step * 2 * rows, rows)
        message[pl.ds(at, rows), :] = queries[place, :]
        message[pl.ds(at + rows, rows), :] = grads[place, :]

    @pl.when(step == heads - 1)
    def _():
        for distance, message in enumerate(messages):
            other = jnp.bitwise_xor(member, distance)
            message[pl.ds(2 * heads * rows, EXT), :] = ext[
                pl.ds(pl.multiple_of(other * EXT, EXT), EXT), :
            ]


def keys_kernel(dims, index, *refs):
    members, rows, _, chips, start, heads = dims
    keys_ref, values_ref, mine_ref, other_ref, keys_grad, values_grad = refs[:6]
    left_ref, right_ref, seed_ref, seed_t_ref = refs[6:10]
    messages = refs[10 : 10 + members]
    dkeys, dvalues, sums_ref = refs[10 + members :]
    step = pl.program_id(0)
    head = step + start
    member = index[0]
    tokens = members * rows
    reach = rows // 2

    @pl.when(step == 0)
    def _():
        assemble_sums(sums_ref, mine_ref, other_ref, index, chips)

    sums = sums_ref[pl.ds(pl.multiple_of(head * 256, 256), 256), :]
    totals = rows_to_column(sums_ref[pl.ds(pl.multiple_of(heads * 256 + head * EXT, EXT), EXT), :])
    normed, scale = normed_t(jnp.transpose(keys_ref[...]))
    feats = features_t(seed_t_ref[...], normed)
    dfeats = mm3_deep(split2(sums), split2(jnp.transpose(values_ref[...]))) + totals
    key_low = normed_grad_t(seed_ref[...], feats, dfeats, normed, scale)
    value_low = mm3_tall(split2(jnp.transpose(sums)), split2(feats))
    dkeys[...] = keys_grad[...] + jnp.transpose(key_low)
    dvalues[...] = values_grad[...] + jnp.transpose(value_low)
    dkeys[:reach] += left_ref[:reach]
    dvalues[:reach] += left_ref[reach:]
    dkeys[tokens - reach :] += right_ref[:reach]
    dvalues[tokens - reach :] += right_ref[reach:]
    for distance, message in enumerate(messages):
        other = jnp.bitwise_xor(member, distance)
        place = pl.ds(pl.multiple_of(other * rows, rows), rows)
        message[:rows] = dkeys[place, :]
        message[rows:] = dvalues[place, :]


def per_head_call(kernel, dims, index, ins, outs, scratch, flops, exps, name):
    heads = dims[2]
    size = sum(math.prod(s.shape) * 4 for s, _ in outs)
    return pl.pallas_call(
        functools.partial(kernel, dims),
        grid_spec=pltpu.PrefetchScalarGridSpec(
            num_scalar_prefetch=1,
            grid=(heads,),
            in_specs=[spec for _, spec in ins],
            out_specs=[spec for _, spec in outs],
            scratch_shapes=scratch,
        ),
        out_shape=[shape for shape, _ in outs],
        compiler_params=pltpu.CompilerParams(
            vmem_limit_bytes=56 * 1024 * 1024, dimension_semantics=("arbitrary",)
        ),
        cost_estimate=pl.CostEstimate(
            flops=flops * heads, bytes_accessed=2 * size, transcendentals=exps * heads
        ),
        name=name,
    )(index, *[x for x, _ in ins])


def swap(block, axis, distance):
    return lax.ppermute(block, axis, [(i, i ^ distance) for i in range(lax.axis_size(axis))])


def cut_sums(index, mine, got):
    chips = lax.axis_size("seq") // 2
    part = jax.ShapeDtypeStruct((mine.shape[0] // chips, 128), F32)
    return pl.pallas_call(
        cut_kernel,
        grid_spec=pltpu.PrefetchScalarGridSpec(
            num_scalar_prefetch=1,
            grid=(1,),
            in_specs=[pl.BlockSpec(mine.shape, lambda i, ref: (0, 0))] * 2,
            out_specs=[pl.BlockSpec(part.shape, lambda i, ref: (0, 0))] * chips,
            scratch_shapes=[pltpu.VMEM(mine.shape, F32)],
        ),
        out_shape=[part] * chips,
        cost_estimate=pl.CostEstimate(
            flops=mine.size, bytes_accessed=12 * mine.size, transcendentals=0
        ),
        name="cut_sums",
    )(index, mine, got)


def reduce_parts(parts):
    own = parts[0]
    for d, part in enumerate(parts[1:], 1):
        own = own + swap(part, "seq", 2 * d)
    return own


def gather_parts(own):
    chips = lax.axis_size("seq") // 2
    return jnp.concatenate([own] + [swap(own, "seq", 2 * d) for d in range(1, chips)], axis=0)


def after(value, *others):
    return lax.optimization_barrier((value, *others))[0]


def to_next(block):
    count = lax.axis_size("seq")
    return lax.ppermute(block, "seq", [(i, i + 1) for i in range(count - 1)])


def to_previous(block):
    count = lax.axis_size("seq")
    return lax.ppermute(block, "seq", [(i + 1, i) for i in range(count - 1)])


def shards(
    queries,
    key_matrix,
    value_matrix,
    gate_logits,
    output_grad,
    cycle_offsets,
    block_count,
    feature_seed,
):
    rows, width = queries.shape
    members = lax.axis_size("blk")
    member = lax.axis_index("blk")
    groups = lax.axis_size("seq")
    group = lax.axis_index("seq")
    chips = groups // 2
    heads = gate_logits.shape[1] // members
    tokens = members * rows
    others = range(1, members)
    index = jnp.stack(
        [
            member,
            (group == 0).astype(jnp.int32),
            (group == groups - 1).astype(jnp.int32),
            group & 1,
            group >> 1,
        ]
    ).astype(jnp.int32)
    sum_rows = -(-(heads * (256 + EXT)) // (EXT * groups)) * EXT * groups
    chunks = [(0, heads // 2), (heads // 2, heads - heads // 2)]
    dims = (members, rows, heads, chips, 0, heads)

    def shape(*sizes):
        return jax.ShapeDtypeStruct(sizes, F32)

    def block_of(message_rows, at):
        return pl.BlockSpec((message_rows, 128), lambda h, ref: (at(h, ref), 0))

    def per_head(block, start=0):
        return pl.BlockSpec(block, lambda h, ref: (h + start, 0))

    def whole(x):
        return pl.BlockSpec(x.shape, lambda h, ref: (0,) * len(x.shape))

    def packing(index, ins, outs, extra):
        moves = []
        for d, out in zip(others, outs):
            other = jnp.bitwise_xor(index[0], d)
            for a in range(2):
                for h in range(heads):
                    column = pl.multiple_of((other * heads + h) * 128, 128)
                    moves.append(
                        (
                            ins[a].at[:, pl.ds(column, 128)],
                            out.at[pl.ds((a * heads + h) * rows, rows), :],
                        )
                    )
            if extra:
                start = pl.multiple_of(other * EXT, EXT)
                moves.append(
                    (ins[2].at[pl.ds(start, EXT), :], out.at[pl.ds(2 * heads * rows, EXT), :])
                )
        return moves

    def unpacking(index, ins, outs):
        moves = []
        for chunk, (start, count) in enumerate(chunks):
            for d in range(members):
                other = jnp.bitwise_xor(index[0], d)
                message = ins[chunk * members + d]
                for a in range(2):
                    for h in range(count):
                        column = pl.multiple_of((other * heads + start + h) * 128, 128)
                        moves.append(
                            (
                                message.at[pl.ds((2 * h + a) * rows, rows), :],
                                outs[a].at[:, pl.ds(column, 128)],
                            )
                        )
        return moves

    kv_sent = tile_copies(
        functools.partial(packing, extra=False),
        2 * heads * (members - 1),
        index,
        [key_matrix, value_matrix],
        [shape(2 * heads * rows, 128)] * (members - 1),
        "pack_kv",
    )
    kv = [swap(block, "blk", d) for d, block in zip(others, kv_sent)]

    active = jnp.arange(cycle_offsets.shape[1], dtype=jnp.int32) < block_count[0]
    named = jnp.mod(cycle_offsets[0] + member, members)
    lanes = jnp.arange(128, dtype=jnp.int32)
    flags = jnp.any(active[:, None] & (named[:, None] == lanes[None, :]), axis=0).astype(F32)
    logits = jnp.transpose(gate_logits).reshape(members, heads, rows)
    ext = jnp.concatenate(
        [
            logits,
            jnp.zeros((members, EXT - 1 - heads, rows), F32),
            jnp.broadcast_to(flags[None, None, :], (members, 1, 128)),
        ],
        axis=1,
    ).reshape(members * EXT, 128)
    qd_sent = local_copies(
        functools.partial(packing, extra=True),
        (2 * heads + 1) * (members - 1),
        index,
        [queries, output_grad, ext],
        [shape(2 * heads * rows + EXT, 128)] * (members - 1),
        "pack_qd",
    )
    kv, qd_sent = lax.optimization_barrier((kv, qd_sent))
    qd = [swap(block, "blk", d) for d, block in zip(others, qd_sent)]

    seed = feature_seed.astype(BF16)
    seed_t = jnp.transpose(feature_seed).astype(BF16)
    unit = 2 * tokens * 128 * 256
    exps = tokens * 256
    half = shape(sum_rows // 2, 128)
    all_sums = pltpu.VMEM((sum_rows, 128), F32)
    own_spec = pl.BlockSpec((rows, 128), lambda h, ref: (0, ref[0] * heads + h))
    keys_full, values_full, sums, sums_other, low_edge, high_edge = per_head_call(
        sums_kernel,
        dims,
        index,
        [(key_matrix, own_spec)]
        + [(x, per_head((rows, 128))) for x in kv]
        + [(value_matrix, own_spec)]
        + [(x, per_head((rows, 128), heads)) for x in kv]
        + [(seed_t, whole(seed_t))],
        [
            (shape(heads * tokens, 128), per_head((tokens, 128))),
            (shape(heads * tokens, 128), per_head((tokens, 128))),
            (half, whole(half)),
            (half, whole(half)),
            (shape(heads * rows, 128), per_head((rows, 128))),
            (shape(heads * rows, 128), per_head((rows, 128))),
        ],
        [all_sums],
        6 * unit,
        exps,
        "key_sums",
    )
    right_halo = to_previous(low_edge)
    left_halo = to_next(high_edge)
    sums = reduce_parts(cut_sums(index, sums, swap(sums_other, "seq", 1)))
    sums, *qd[:2] = lax.optimization_barrier((sums, *qd[:2]))
    sums = gather_parts(sums)
    sums_other = swap(sums, "seq", 1)

    ext_block = block_of(EXT, lambda h, ref: 2 * heads * rows // EXT)

    def query_side(start):
        own = pl.BlockSpec((rows, 128), lambda h, ref: (0, ref[0] * heads + start + h))
        return (
            [(queries, own)]
            + [(x, per_head((rows, 128), start)) for x in qd]
            + [(output_grad, own)]
            + [(x, per_head((rows, 128), heads + start)) for x in qd]
            + [(ext, block_of(EXT, lambda h, ref: ref[0]))]
            + [(x, ext_block) for x in qd]
        )

    row_scratch = [
        pltpu.VMEM((tokens, 128), F32),
        pltpu.VMEM((tokens, 128), F32),
        pltpu.VMEM((members * EXT, 128), F32),
    ]
    low, query_low, sums_grad, grad_other = per_head_call(
        query_kernel,
        dims,
        index,
        query_side(0)
        + [
            (sums, whole(sums)),
            (sums_other, whole(sums_other)),
            (seed, whole(seed)),
            (seed_t, whole(seed_t)),
        ],
        [
            (shape(heads * 128, tokens), per_head((128, tokens))),
            (shape(heads * 128, tokens), per_head((128, tokens))),
            (half, whole(half)),
            (half, whole(half)),
        ],
        row_scratch + [all_sums, all_sums],
        14 * unit,
        exps,
        "query_low_rank",
    )

    def sparse(chunk, low, query_low):
        start, count = chunks[chunk]
        message = shape(2 * count * rows + EXT, 128)
        outs = per_head_call(
            sparse_kernel,
            (members, rows, count, chips, start, heads),
            index,
            query_side(start)
            + [
                (keys_full, per_head((tokens, 128), start)),
                (values_full, per_head((tokens, 128), start)),
                (left_halo, per_head((rows, 128), start)),
                (right_halo, per_head((rows, 128), start)),
                (low, per_head((128, tokens), start)),
                (query_low, per_head((128, tokens), start)),
            ],
            [(message, whole(message))] * members
            + [(shape(count * tokens, 128), per_head((tokens, 128)))] * 2
            + [(shape(count * rows, 128), per_head((rows, 128)))] * 2,
            row_scratch
            + [
                pltpu.VMEM((tokens + rows, tokens), F32),
                pltpu.VMEM((tokens + rows, 128), F32),
                pltpu.VMEM((tokens + rows, 128), F32),
            ],
            42 * tokens * (tokens + rows) * 128,
            tokens * (tokens + rows),
            "sparse",
        )
        return outs[:members], outs[members:]

    def key_side(chunk, parts, sums, sums_other):
        start, count = chunks[chunk]
        keys_sparse, values_sparse, left_grad, right_grad = parts
        back_right = to_previous(left_grad)
        back_left = to_next(right_grad)
        message = shape(2 * count * rows, 128)
        return per_head_call(
            keys_kernel,
            (members, rows, count, chips, start, heads),
            index,
            [
                (keys_full, per_head((tokens, 128), start)),
                (values_full, per_head((tokens, 128), start)),
                (sums, whole(sums)),
                (sums_other, whole(sums_other)),
                (keys_sparse, per_head((tokens, 128))),
                (values_sparse, per_head((tokens, 128))),
                (back_left, per_head((rows, 128))),
                (back_right, per_head((rows, 128))),
                (seed, whole(seed)),
                (seed_t, whole(seed_t)),
            ],
            [(message, per_head((2 * rows, 128)))] * members,
            [pltpu.VMEM((tokens, 128), F32), pltpu.VMEM((tokens, 128), F32), all_sums],
            13 * unit,
            exps,
            "key_low_rank",
        )

    def back(messages):
        return [messages[0]] + [swap(block, "blk", d) for d, block in zip(others, messages[1:])]

    parts = cut_sums(index, sums_grad, swap(grad_other, "seq", 1))
    low, query_low, *parts = lax.optimization_barrier((low, query_low, *parts))
    od_first, keys_first = sparse(0, low, query_low)
    own = reduce_parts(parts)
    low, query_low, own, *od_first = lax.optimization_barrier((low, query_low, own, *od_first))
    od_first = back(od_first)
    od_second, keys_second = sparse(1, low, query_low)
    sums = gather_parts(own)
    sums, *od_second = lax.optimization_barrier((sums, *od_second))
    sums_other = swap(sums, "seq", 1)
    od_second = back(od_second)
    dkv_first = back(key_side(0, keys_first, sums, sums_other))
    dkv_second = back(key_side(1, keys_second, sums, sums_other))

    od = od_first + od_second
    n_moves = 2 * heads * members
    attended, query_grad = local_copies(
        unpacking, n_moves, index, od, [shape(rows, width)] * 2, "unpack_od"
    )
    gate_parts = []
    for chunk, (start, count) in enumerate(chunks):
        rows_back = jnp.zeros((members, EXT, 128), F32)
        for d in range(members):
            block = od[chunk * members + d]
            rows_back = lax.dynamic_update_slice_in_dim(
                rows_back, block[None, 2 * count * rows :, :], member ^ d, 0
            )
        gate_parts.append(rows_back[:, start : start + count, :])
    gate_grad = jnp.concatenate(gate_parts, axis=1).reshape(members * heads, rows)
    key_grad, value_grad = local_copies(
        unpacking,
        n_moves,
        index,
        dkv_first + dkv_second,
        [shape(rows, width)] * 2,
        "unpack_kv",
    )
    return (attended, query_grad, key_grad, value_grad, jnp.transpose(gate_grad))


def solution(mesh):
    row_spec = P(("seq", "blk"), None)
    return jax.shard_map(
        shards,
        mesh=mesh,
        in_specs=(row_spec,) * 6 + (P(("seq", "blk")), P()),
        out_specs=(row_spec,) * 5,
        check_vma=False,
    )
```
